32 devices in a mesh: section: 2 (over core), seq: 4 (over z), fsdp: 4 (over y, x).
Axes of the slice: x: 2, y: 2, z: 4, core: 2. Of those that a mesh axis runs over, the one named last changes fastest.
Arguments:
- activations: bfloat16 [2, 4, 1024, 1024], P(None, 'fsdp', 'seq'), may hold values from -6 to 6
- cotangent: bfloat16 [2, 4, 1024, 1024], P(None, 'fsdp', 'seq'), may hold values from -6 to 6
- lengths: int32 [2, 4], P(None, 'fsdp'), may hold values from 896 to 1024, as said below
- mixgain: bfloat16 [2, 1024], P('section', 'fsdp'), may hold values from 0.5 to 1.5
- mixshift: bfloat16 [2, 1024], P('section', 'fsdp'), may hold values from -1.75 to 1.75
- mixweight: bfloat16 [2, 1024, 3072], P('section', 'fsdp'), may hold values from -0.25 to 0.25
- mixbias: bfloat16 [2, 2, 1024], P('section', None, 'fsdp'), may hold values from -1.75 to 1.75
- outweight: bfloat16 [2, 1024, 1024], P('section', 'fsdp'), may hold values from -0.75 to 0.75
- outbias: bfloat16 [2, 1024], P('section', 'fsdp'), may hold values from -1.75 to 1.75
- mixscale: bfloat16 [2, 1024], P('section', 'fsdp'), may hold values from 0.5 to 2
- feedgain: bfloat16 [2, 1024], P('section', 'fsdp'), may hold values from 0.5 to 1.5
- feedshift: bfloat16 [2, 1024], P('section', 'fsdp'), may hold values from -1.75 to 1.75
- upweight: bfloat16 [2, 1024, 4096], P('section', 'fsdp'), may hold values from -0.1875 to 0.1875
- upbias: bfloat16 [2, 4096], P('section', 'fsdp'), may hold values from -1.75 to 1.75
- downweight: bfloat16 [2, 4096, 1024], P('section', 'fsdp'), may hold values from -0.09375 to 0.09375
- downbias: bfloat16 [2, 1024], P('section', 'fsdp'), may hold values from -1.75 to 1.75
- feedscale: bfloat16 [2, 1024], P('section', 'fsdp'), may hold values from 0.5 to 2
Outputs:
- section_output: bfloat16 [2, 2, 4, 1024, 1024], P('section', None, 'fsdp', 'seq')
- input_gradient: float32 [2, 2, 4, 1024, 1024], P('section', None, 'fsdp', 'seq')
- mixgain_gradient: float32 [2, 1024], P('section', 'fsdp')
- mixshift_gradient: float32 [2, 1024], P('section', 'fsdp')
- mixweight_gradient: float32 [2, 1024, 3072], P('section', 'fsdp')
- mixbias_gradient: float32 [2, 2, 1024], P('section', None, 'fsdp')
- outweight_gradient: float32 [2, 1024, 1024], P('section', 'fsdp')
- outbias_gradient: float32 [2, 1024], P('section', 'fsdp')
- mixscale_gradient: float32 [2, 1024], P('section', 'fsdp')
- feedgain_gradient: float32 [2, 1024], P('section', 'fsdp')
- feedshift_gradient: float32 [2, 1024], P('section', 'fsdp')
- upweight_gradient: float32 [2, 1024, 4096], P('section', 'fsdp')
- upbias_gradient: float32 [2, 4096], P('section', 'fsdp')
- downweight_gradient: float32 [2, 4096, 1024], P('section', 'fsdp')
- downbias_gradient: float32 [2, 1024], P('section', 'fsdp')
- feedscale_gradient: float32 [2, 1024], P('section', 'fsdp')
The draws below stay inside these ranges and needn't reach their ends.
Inputs may be any that keep to these rules, and one draw needn't show every extreme that they name: `lengths`: each micro-batch has one image, drawn from the seed, of length 1024; keys at or past an image's length are masked.
All inputs are finite; a program needn't handle non-finite values.
Results may differ from the reference program's by a relative error of at most 0.019.
Values may be sent and summed in bfloat16 or wider, within the bound.
No kernel may reach another device: no remote copies, remote signals or barrier semaphores. Data moves between devices by JAX's collectives and lax.ppermute only.
A program may use at most 256 MiB of HBM per device.

```python
import math
import jax
import jax.numpy as jnp
from jax import lax

D = 1024
HEADS = 16
HEAD_DIM = 64
FF = 4096
LEN = 1024
MICRO = 2
IMAGES = 4
SECTIONS = 2


def draw_lengths(key, part):
    key = jax.random.fold_in(key, 7)
    first_key, second_key = jax.random.split(key)
    drawn_lengths = jax.random.randint(first_key, (MICRO, IMAGES), LEN - LEN // 8, LEN + 1)
    chosen = jax.random.randint(second_key, (MICRO, 1), 0, IMAGES)
    whole_image = jnp.arange(IMAGES)[None, :] == chosen
    return jnp.where(whole_image, LEN, drawn_lengths).astype(jnp.int32)


def block_scale(key, extent, shards, low, top_value):
    level, own = 1.0, jax.random.fold_in(key, 6)
    for position, shards_of in shards:
        draws = jnp.exp(jax.random.uniform(jax.random.fold_in(own, position), (shards_of,), jnp.float32, low / len(shards), top_value / len(shards)))
        level = level * jnp.repeat(draws, extent[position] // shards_of).reshape([-1 if axis == position else 1 for axis in range(len(extent))])
    return level


def bell_draw(stream_key, extent, width, bound, shards=(), kind=jnp.bfloat16):
    level = block_scale(stream_key, extent, shards, -0.22, 0.18) if shards else 1.0
    drawn = jax.random.normal(stream_key, extent, jnp.float32) * width * level
    return jnp.minimum(jnp.maximum(drawn, -bound), bound).astype(kind)


def setup_inputs(seed: int = 0) -> dict:
    key_of = jax.random.split(jax.random.key(seed), 18)
    return {
        "activations": bell_draw(key_of[0], (MICRO, IMAGES, LEN, D), 1.0, 6.0, ((1, 4), (2, 4))),
        "cotangent": bell_draw(key_of[1], (MICRO, IMAGES, LEN, D), 1.0, 6.0, ((1, 4), (2, 4))),
        "lengths": draw_lengths(jax.random.fold_in(key_of[17], 71), 0),
        "mixgain": jnp.clip(1.0 + 0.1 * jax.random.normal(key_of[3], (SECTIONS, D), jnp.float32), 0.5, 1.5).astype(jnp.bfloat16),
        "mixshift": bell_draw(key_of[4], (SECTIONS, D), 0.3, 1.75, ((0, 2), (1, 4))),
        "mixweight": bell_draw(key_of[5], (SECTIONS, D, 3 * D), (D // 2) ** -0.5, 0.25, ((0, 2), (1, 4))),
        "mixbias": bell_draw(key_of[6], (SECTIONS, 2, D), 0.3, 1.75, ((0, 2), (2, 4))),
        "outweight": bell_draw(key_of[7], (SECTIONS, D, D), (D // 16) ** -0.5, 0.75, ((0, 2), (1, 4))),
        "outbias": bell_draw(key_of[8], (SECTIONS, D), 0.3, 1.75, ((0, 2), (1, 4))),
        "mixscale": jnp.clip(jnp.exp(math.log(2.0) - 1.3862944 * jax.random.uniform(key_of[9], (SECTIONS, D), jnp.float32) ** block_scale(key_of[9], (SECTIONS, D), ((0, 2), (1, 4)), -0.2, 0.2)), 0.5, 2.0).astype(jnp.bfloat16),
        "feedgain": jnp.clip(1.0 + 0.1 * jax.random.normal(key_of[10], (SECTIONS, D), jnp.float32), 0.5, 1.5).astype(jnp.bfloat16),
        "feedshift": bell_draw(key_of[11], (SECTIONS, D), 0.3, 1.75, ((0, 2), (1, 4))),
        "upweight": bell_draw(key_of[12], (SECTIONS, D, FF), D ** -0.5, 0.1875, ((0, 2), (1, 4))),
        "upbias": bell_draw(key_of[13], (SECTIONS, FF), 0.3, 1.75, ((0, 2), (1, 4))),
        "downweight": bell_draw(key_of[14], (SECTIONS, FF, D), FF ** -0.5, 0.09375, ((0, 2), (1, 4))),
        "downbias": bell_draw(key_of[15], (SECTIONS, D), 0.3, 1.75, ((0, 2), (1, 4))),
        "feedscale": jnp.clip(jnp.exp(math.log(2.0) - 1.3862944 * jax.random.uniform(key_of[16], (SECTIONS, D), jnp.float32) ** block_scale(key_of[16], (SECTIONS, D), ((0, 2), (1, 4)), -0.2, 0.2)), 0.5, 2.0).astype(jnp.bfloat16),
    }


@jax.custom_vjp
def low(v):
    return lax.optimization_barrier(v.astype(jnp.bfloat16)).astype(jnp.float32)

@jax.custom_vjp
def low_back(v):
    return v

def low_keep(v):
    return (low(v), None)

def low_pass(kept, grad):
    return (grad,)

def back_keep(v):
    return (v, None)

def back_low(kept, grad):
    return (low(grad),)
low.defvjp(low_keep, low_pass)
low_back.defvjp(back_keep, back_low)
EPSILON = 1e-06
NEGATIVE = -1000000000.0
HIGHEST = lax.Precision.HIGHEST

def norm_apply(values, gain, shift):
    center = lax.optimization_barrier(jnp.mean(values, axis=-1, keepdims=True))
    centered = values - center
    spread = lax.optimization_barrier(jnp.mean(centered * centered, axis=-1, keepdims=True))
    return centered * lax.rsqrt(spread + EPSILON) * gain + shift

def product(operand, matrix):
    return jnp.dot(operand, matrix, precision=HIGHEST, preferred_element_type=jnp.float32)

def image_layer(params, hidden, length):
    mixgain, mixshift, mixweight, mixbias, outweight, outbias, mixscale, feedgain, feedshift, upweight, upbias, downweight, downbias, feedscale = params
    normed = low(norm_apply(hidden, mixgain, mixshift))
    zeros_row = jnp.zeros_like(mixbias[0])
    triple = product(normed, mixweight) + jnp.concatenate([mixbias[0], zeros_row, mixbias[1]])
    triple = low_back(low(triple)).reshape(LEN, 3, HEADS, HEAD_DIM)
    scores = jnp.einsum('qhd,khd->hqk', triple[:, 0], triple[:, 1], precision=HIGHEST) * HEAD_DIM ** (-0.5)
    key_mask = jnp.arange(LEN) < length
    scores = low_back(jnp.where(key_mask[None, None, :], scores, NEGATIVE))
    probs = low(jax.nn.softmax(scores, axis=-1))
    mixed_heads = jnp.einsum('hqk,khd->qhd', probs, triple[:, 2], precision=HIGHEST).reshape(LEN, D)
    mixed_heads = low_back(low(mixed_heads))
    branch = low_back(product(mixed_heads, outweight) + outbias)
    residual = hidden + mixscale * branch
    normed_two = low(norm_apply(residual, feedgain, feedshift))
    hidden_up = low_back(product(normed_two, upweight) + upbias)
    active = low(jax.nn.gelu(hidden_up, approximate=False))
    branch_two = low_back(product(active, downweight) + downbias)
    return low(residual + feedscale * branch_two)

def section_apply(hidden, lengths, params):
    layer = jax.checkpoint(image_layer)
    return lax.map(lambda paired: layer(params, paired[0], paired[1]), (hidden, lengths))

def both_sections(first_value, second_value):
    return jnp.stack([first_value, second_value]).astype(jnp.float32)

def reference(activations, cotangent, lengths, mixgain, mixshift, mixweight, mixbias, outweight, outbias, mixscale, feedgain, feedshift, upweight, upbias, downweight, downbias, feedscale):
    weights = (mixgain, mixshift, mixweight, mixbias, outweight, outbias, mixscale, feedgain, feedshift, upweight, upbias, downweight, downbias, feedscale)
    first_params = tuple((weight_array[0].astype(jnp.float32) for weight_array in weights))
    second_params = tuple((weight_array[1].astype(jnp.float32) for weight_array in weights))
    inputs = activations.astype(jnp.float32).reshape(MICRO * IMAGES, LEN, D)
    flat_lengths = lengths.reshape(MICRO * IMAGES).astype(jnp.int32)

    def run_section(hidden, params):
        return section_apply(hidden, flat_lengths, params)
    middle, back_first = jax.vjp(run_section, inputs, first_params)
    final_output, back_second = jax.vjp(run_section, middle, second_params)
    middle_grad, second_grads = back_second(cotangent.astype(jnp.float32).reshape(MICRO * IMAGES, LEN, D))
    input_grad, first_grads = back_first(low(middle_grad))
    full_shape = (2, MICRO, IMAGES, LEN, D)
    return (jnp.stack([middle, final_output]).reshape(full_shape).astype(jnp.bfloat16), jnp.stack([input_grad, middle_grad]).reshape(full_shape).astype(jnp.float32), both_sections(first_grads[0], second_grads[0]), both_sections(first_grads[1], second_grads[1]), both_sections(first_grads[2], second_grads[2]), both_sections(first_grads[3], second_grads[3]), both_sections(first_grads[4], second_grads[4]), both_sections(first_grads[5], second_grads[5]), both_sections(first_grads[6], second_grads[6]), both_sections(first_grads[7], second_grads[7]), both_sections(first_grads[8], second_grads[8]), both_sections(first_grads[9], second_grads[9]), both_sections(first_grads[10], second_grads[10]), both_sections(first_grads[11], second_grads[11]), both_sections(first_grads[12], second_grads[12]), both_sections(first_grads[13], second_grads[13]))
```

```python
import math

import jax
import jax.numpy as jnp
from jax import lax
from jax.experimental import pallas as pl
from jax.experimental.pallas import tpu as pltpu
from jax.sharding import PartitionSpec as P

HEAD_DIM = 64
EPSILON = 1e-06
NEGATIVE = -1000000000.0
F32 = jnp.float32
BF16 = jnp.bfloat16
GROUP = 256
MIN_LENGTH = 896
CHUNK = 256
ROWS = 64
MIB = 1024 * 1024


def dot_nn(left, right):
    return lax.dot_general(left, right, (((1,), (0,)), ((), ())), preferred_element_type=F32)


def dot_nt(left, right):
    return lax.dot_general(left, right, (((1,), (1,)), ((), ())), preferred_element_type=F32)


def dot_tn(left, right):
    return lax.dot_general(left, right, (((0,), (0,)), ((), ())), preferred_element_type=F32)


def size_of(shape, dtype):
    return math.prod(shape) * jnp.dtype(dtype).itemsize


def run_kernel(body, name, ins, outs, scratch, flops, exps=0):
    spaces = {"v": pltpu.VMEM, "a": pl.ANY, "s": pltpu.SMEM}
    moved = sum(size_of(a.shape, a.dtype) for a, _ in ins) + sum(size_of(s, d) for s, d, _ in outs)
    held = sum(size_of(a.shape, a.dtype) for a, k in ins if k == "v")
    held += sum(size_of(s, d) for s, d, k in outs if k == "v")
    held += sum(size_of(s.shape, s.dtype) for s in scratch if s.memory_space == pltpu.VMEM)
    return pl.pallas_call(
        body,
        name=name,
        out_shape=[jax.ShapeDtypeStruct(s, d) for s, d, _ in outs],
        in_specs=[pl.BlockSpec(memory_space=spaces[k]) for _, k in ins],
        out_specs=[pl.BlockSpec(memory_space=spaces[k]) for _, _, k in outs],
        scratch_shapes=scratch,
        compiler_params=pltpu.CompilerParams(vmem_limit_bytes=min(held + 14 * MIB, 58 * MIB)),
        cost_estimate=pl.CostEstimate(flops=flops, bytes_accessed=moved, transcendentals=exps),
    )(*[a for a, _ in ins])


def start_all(pairs, sems, first=0):
    copies = []
    for index, (source, target) in enumerate(pairs):
        copies.append(pltpu.make_async_copy(source, target, sems.at[first + index]))
        copies[-1].start()
    return copies


def wait_all(copies):
    for copy in copies:
        copy.wait()


def block_rows(scal, k, rows):
    return pl.ds(pl.multiple_of((scal[0] ^ k) * rows, rows), rows)


def mix_pairs(scal, pieces, full, rows, count):
    return [
        (
            pieces[2 * k + h].at[t * rows : (t + 1) * rows, :],
            full.at[block_rows(scal, k, rows), (3 * h + t) * GROUP : (3 * h + t + 1) * GROUP],
        )
        for k in range(count)
        for h in range(2)
        for t in range(3)
    ]


def out_pairs(scal, pieces, full, rows, count):
    half = rows // 2
    return [
        (
            pieces[2 * k + h].at[3 * rows + j * half : 3 * rows + (j + 1) * half, :],
            full.at[block_rows(scal, k, half), (2 * h + j) * GROUP : (2 * h + j + 1) * GROUP],
        )
        for k in range(count)
        for h in range(2)
        for j in range(2)
    ]


def up_pairs(scal, pieces, full, rows, count):
    width = pieces[0].shape[1]
    return [
        (
            pieces[2 * k + h].at[j * rows : (j + 1) * rows, :],
            full.at[block_rows(scal, k, rows), (2 * h + j) * width : (2 * h + j + 1) * width],
        )
        for k in range(count)
        for h in range(2)
        for j in range(2)
    ]


def down_pairs(scal, pieces, full, rows, count):
    width = pieces[0].shape[1]
    return [
        (
            pieces[2 * k + h].at[2 * rows : 4 * rows, :],
            full.at[block_rows(scal, k, 2 * rows), h * width : (h + 1) * width],
        )
        for k in range(count)
        for h in range(2)
    ]


def norm_parts(values):
    center = jnp.mean(values, axis=-1, keepdims=True)
    centered = values - center
    spread = jnp.mean(centered * centered, axis=-1, keepdims=True)
    inverse = lax.rsqrt(spread + EPSILON)
    return centered * inverse, inverse


def norm_back(values, gain, grad):
    unit, inverse = norm_parts(values)
    scaled = grad * gain
    mean_one = jnp.mean(scaled, axis=-1, keepdims=True)
    mean_two = jnp.mean(scaled * unit, axis=-1, keepdims=True)
    return inverse * (scaled - mean_one - unit * mean_two), unit


def column_sum(values):
    return jnp.sum(values, axis=0, keepdims=True)


def gelu_pair(values):
    energy = jnp.exp(values * values * -0.5)
    t = 1.0 / (1.0 + (0.3275911 * 0.7071067811865476) * jnp.abs(values))
    tail = 1.061405429 * 0.5
    for factor in (-1.453152027, 1.421413741, -0.284496736, 0.254829592):
        tail = tail * t + factor * 0.5
    tail = tail * t * energy
    below = jnp.where(values >= 0, 1.0 - tail, tail)
    return values * below, below + values * energy * 0.3989422804014327


def mix_forward(params, hidden, gain, shift, bias, scal, pieces):
    rows, count = params
    tokens, width = hidden.shape
    span = 3 * GROUP

    def body(scal, hidden, gain, shift, bias, *rest):
        pieces, (normed, keep, send, full, sems) = rest[: 2 * count], rest[2 * count :]
        copies = start_all(mix_pairs(scal, pieces, full, rows, count), sems)

        @pl.loop(0, tokens // ROWS)
        def _(i):
            part = pl.ds(pl.multiple_of(i * ROWS, ROWS), ROWS)
            unit, _ = norm_parts(hidden[part, :].astype(F32))
            normed[part, :] = (unit * gain[...] + shift[...]).astype(BF16)

        wait_all(copies)
        for target, group in ((send, 1 - scal[1]), (keep, scal[1])):
            for t in range(3):
                columns = pl.ds(pl.multiple_of((group * 3 + t) * GROUP, GROUP), GROUP)
                made = dot_nn(normed[...], full[:, columns]) + bias[:, columns]
                target[:, t * GROUP : (t + 1) * GROUP] = made.astype(BF16)

    return run_kernel(
        body,
        "mix_forward",
        [(scal, "s"), (hidden, "v"), (gain, "v"), (shift, "v"), (bias, "v")]
        + [(p, "a") for p in pieces],
        [((tokens, width), BF16, "v"), ((tokens, span), BF16, "v"), ((tokens, span), BF16, "v")],
        [pltpu.VMEM((width, 2 * span), BF16), pltpu.SemaphoreType.DMA((6 * count,))],
        4 * tokens * width * span,
    )


def place_tokens(scal, keep, other, full, sems, first=0):
    tokens = keep.shape[0]
    own = pl.ds(pl.multiple_of(scal[1] * tokens, tokens), tokens)
    far = pl.ds(pl.multiple_of((1 - scal[1]) * tokens, tokens), tokens)
    return start_all([(keep, full.at[own, :]), (other, full.at[far, :])], sems, first)


def split_tokens(scal, full, keep, send, sems):
    tokens = keep.shape[0]
    own = pl.ds(pl.multiple_of(scal[1] * tokens, tokens), tokens)
    far = pl.ds(pl.multiple_of((1 - scal[1]) * tokens, tokens), tokens)
    wait_all(start_all([(full.at[far, :], send), (full.at[own, :], keep)], sems))


def masked(scores, length):
    start = MIN_LENGTH
    tail = scores[start:, :]
    position = lax.broadcasted_iota(jnp.int32, tail.shape, 0) + start
    return scores[:start, :], jnp.where(position < length, tail, NEGATIVE)


def attend_forward(keep, other, scal):
    tokens = keep.shape[0]
    total = 2 * tokens
    heads = GROUP // HEAD_DIM

    def body(scal, keep, other, out_keep, out_send, peaks, full, out, sems):
        wait_all(place_tokens(scal, keep, other, full, sems))
        length = scal[2]
        for pair in range(heads // 2):

            @pl.loop(0, total // CHUNK)
            def _(i):
                part = pl.ds(pl.multiple_of(i * CHUNK, CHUNK), CHUNK)
                outs = []
                for head in (2 * pair, 2 * pair + 1):
                    at = head * HEAD_DIM
                    query = full[part, at : at + HEAD_DIM] * jnp.asarray(HEAD_DIM**-0.5, BF16)
                    key = full[:, GROUP + at : GROUP + at + HEAD_DIM]
                    value = full[:, 2 * GROUP + at : 2 * GROUP + at + HEAD_DIM]
                    low, high = masked(dot_nt(key, query), length)
                    peak = jnp.maximum(
                        jnp.max(low, axis=0, keepdims=True), jnp.max(high, axis=0, keepdims=True)
                    )
                    low = jnp.exp(low - peak)
                    high = jnp.exp(high - peak)
                    mass = column_sum(low) + column_sum(high)
                    probs = jnp.concatenate([low.astype(BF16), high.astype(BF16)], axis=0)
                    outs.append(dot_tn(value, probs) / mass)
                    peaks[head : head + 1, part] = peak + jnp.log(mass)
                made = jnp.concatenate(outs, axis=0)
                out[part, pair * 128 : (pair + 1) * 128] = made.T.astype(BF16)

        split_tokens(scal, out, out_keep, out_send, sems)

    return run_kernel(
        body,
        "attend_forward",
        [(scal, "s"), (keep, "a"), (other, "a")],
        [
            ((tokens, GROUP), BF16, "a"),
            ((tokens, GROUP), BF16, "a"),
            ((8, total), F32, "v"),
        ],
        [
            pltpu.VMEM((total, 3 * GROUP), BF16),
            pltpu.VMEM((total, GROUP), BF16),
            pltpu.SemaphoreType.DMA((2,)),
        ],
        heads * total * total * HEAD_DIM * 4,
        heads * total * total,
    )


def place_groups(scal, keep, other, full, sems, first=0):
    width = keep.shape[1]
    own = pl.ds(pl.multiple_of(scal[1] * width, width), width)
    far = pl.ds(pl.multiple_of((1 - scal[1]) * width, width), width)
    return start_all([(keep, full.at[:, own]), (other, full.at[:, far])], sems, first)


def out_forward(params, keep, other, scal, pieces, width):
    rows, count = params
    tokens = keep.shape[0]
    inner = 2 * GROUP

    def body(scal, keep, other, *rest):
        pieces, (mixed, own, send, full, sems) = rest[: 2 * count], rest[2 * count :]
        copies = place_groups(scal, keep, other, mixed, sems)
        copies += start_all(out_pairs(scal, pieces, full, rows, count), sems, 2)
        wait_all(copies)
        for j in range(width // GROUP):
            columns = slice(j * GROUP, (j + 1) * GROUP)
            made = dot_nn(mixed[...], full[:, columns])
            own[:, columns] = made
            send[:, columns] = made.astype(BF16)

    return run_kernel(
        body,
        "out_forward",
        [(scal, "s"), (keep, "a"), (other, "a")] + [(p, "a") for p in pieces],
        [((tokens, inner), BF16, "v"), ((tokens, width), F32, "v"), ((tokens, width), BF16, "v")],
        [pltpu.VMEM((inner, width), BF16), pltpu.SemaphoreType.DMA((4 * count + 2,))],
        2 * tokens * inner * width,
    )


def feed_forward(params, hidden, own, other, vectors, upbias, scal, pieces):
    rows, count = params
    tokens, width = hidden.shape
    inner = upbias.shape[1]
    tile = 512

    def body(scal, hidden, own, other, vectors, upbias, *rest):
        pieces = rest[: 2 * count]
        branch, residual, normed, active, slope, made_own, made_send, up, down, sems = rest[
            2 * count :
        ]
        up_copies = start_all(up_pairs(scal, pieces, up, rows, count), sems)
        down_copies = start_all(down_pairs(scal, pieces, down, rows, count), sems, 4 * count)

        @pl.loop(0, tokens // ROWS)
        def _(i):
            part = pl.ds(pl.multiple_of(i * ROWS, ROWS), ROWS)
            made = own[part, :] + other[part, :].astype(F32) + vectors[0:1, :]
            branch[part, :] = made
            made = hidden[part, :].astype(F32) + vectors[1:2, :] * made
            residual[part, :] = made
            unit, _ = norm_parts(made)
            normed[part, :] = (unit * vectors[2:3, :] + vectors[3:4, :]).astype(BF16)

        wait_all(up_copies)

        @pl.loop(0, inner // tile)
        def _(i):
            columns = pl.ds(pl.multiple_of(i * tile, tile), tile)
            for r in range(tokens // 256):
                part = slice(r * 256, (r + 1) * 256)
                made = dot_nn(normed[part, :], up[:, columns]) + upbias[:, columns]
                value, gradient = gelu_pair(made)
                active[part, columns] = value.astype(BF16)
                slope[part, columns] = gradient.astype(BF16)

        wait_all(down_copies)

        @pl.loop(0, width // GROUP)
        def _(i):
            columns = pl.ds(pl.multiple_of(i * GROUP, GROUP), GROUP)
            made = dot_nn(active[...], down[:, columns])
            made_own[:, columns] = made
            made_send[:, columns] = made.astype(BF16)

    return run_kernel(
        body,
        "feed_forward",
        [(scal, "s"), (hidden, "v"), (own, "v"), (other, "v"), (vectors, "v"), (upbias, "v")]
        + [(p, "a") for p in pieces],
        [
            ((tokens, width), F32, "v"),
            ((tokens, width), F32, "v"),
            ((tokens, width), BF16, "v"),
            ((tokens, inner), BF16, "v"),
            ((tokens, inner), BF16, "v"),
            ((tokens, width), F32, "v"),
            ((tokens, width), BF16, "v"),
        ],
        [
            pltpu.VMEM((width, inner), BF16),
            pltpu.VMEM((inner, width), BF16),
            pltpu.SemaphoreType.DMA((6 * count,)),
        ],
        4 * tokens * width * inner,
        2 * tokens * inner,
    )


def feed_backward(params, incoming, feedscale, slope, scal, pieces):
    rows, count = params
    tokens, width = incoming.shape
    inner = slope.shape[1]
    tile = 512

    def body(scal, incoming, feedscale, slope, *rest):
        pieces = rest[: 2 * count]
        lower, up_grad, bias_grad, made_own, made_send, up, down, sems = rest[2 * count :]
        down_copies = start_all(down_pairs(scal, pieces, down, rows, count), sems)
        up_copies = start_all(up_pairs(scal, pieces, up, rows, count), sems, 2 * count)

        @pl.loop(0, tokens // ROWS)
        def _(i):
            part = pl.ds(pl.multiple_of(i * ROWS, ROWS), ROWS)
            lower[part, :] = (incoming[part, :].astype(F32) * feedscale[...]).astype(BF16)

        wait_all(down_copies)

        @pl.loop(0, inner // tile)
        def _(i):
            columns = pl.ds(pl.multiple_of(i * tile, tile), tile)
            made = dot_nt(lower[...], down[columns, :])
            made = (made * slope[:, columns].astype(F32)).astype(BF16)
            up_grad[:, columns] = made
            bias_grad[:, columns] = column_sum(made.astype(F32))

        wait_all(up_copies)

        @pl.loop(0, width // GROUP)
        def _(i):
            columns = pl.ds(pl.multiple_of(i * GROUP, GROUP), GROUP)
            made = dot_nt(up_grad[...], up[columns, :])
            made_own[:, columns] = made
            made_send[:, columns] = made.astype(BF16)

    return run_kernel(
        body,
        "feed_backward",
        [(scal, "s"), (incoming, "v"), (feedscale, "v"), (slope, "v")]
        + [(p, "a") for p in pieces],
        [
            ((tokens, width), BF16, "v"),
            ((tokens, inner), BF16, "v"),
            ((1, inner), F32, "v"),
            ((tokens, width), F32, "v"),
            ((tokens, width), BF16, "v"),
        ],
        [
            pltpu.VMEM((width, inner), BF16),
            pltpu.VMEM((inner, width), BF16),
            pltpu.SemaphoreType.DMA((6 * count,)),
        ],
        4 * tokens * width * inner,
    )


def feed_weights(params, active, lower, normed, up_grad, scal):
    rows, count = params
    tokens, width = lower.shape
    inner = active.shape[1]
    shape = (4 * rows, inner // 4)
    tile = 512

    def body(scal, active, lower, normed, up_grad, *rest):
        pieces, (up, down, sems) = rest[: 2 * count], rest[2 * count :]

        @pl.loop(0, inner // tile)
        def _(i):
            part = pl.ds(pl.multiple_of(i * tile, tile), tile)
            down[part, :] = dot_tn(active[:, part], lower[...]).astype(BF16)

        pairs = [(b, a) for a, b in down_pairs(scal, pieces, down, rows, count)]
        copies = start_all(pairs, sems)

        @pl.loop(0, inner // tile)
        def _(i):
            part = pl.ds(pl.multiple_of(i * tile, tile), tile)
            up[:, part] = dot_tn(normed[...], up_grad[:, part]).astype(BF16)

        pairs = [(b, a) for a, b in up_pairs(scal, pieces, up, rows, count)]
        wait_all(copies + start_all(pairs, sems, 2 * count))

    return run_kernel(
        body,
        "feed_weights",
        [(scal, "s"), (active, "v"), (lower, "v"), (normed, "v"), (up_grad, "v")],
        [(shape, BF16, "a")] * (2 * count),
        [
            pltpu.VMEM((width, inner), BF16),
            pltpu.VMEM((inner, width), BF16),
            pltpu.SemaphoreType.DMA((6 * count,)),
        ],
        4 * tokens * width * inner,
    )


def feed_sums(incoming, own, other, downbias, lower):
    tokens, width = incoming.shape

    def body(incoming, own, other, downbias, lower, sums):
        sums[...] = jnp.zeros_like(sums)

        @pl.loop(0, tokens // ROWS)
        def _(i):
            part = pl.ds(pl.multiple_of(i * ROWS, ROWS), ROWS)
            branch = own[part, :] + other[part, :].astype(F32) + downbias[...]
            sums[0:1, :] += column_sum(branch * incoming[part, :].astype(F32))
            sums[1:2, :] += column_sum(lower[part, :].astype(F32))

    return run_kernel(
        body,
        "feed_sums",
        [(incoming, "v"), (own, "v"), (other, "v"), (downbias, "v"), (lower, "v")],
        [((8, width), F32, "v")],
        [],
        4 * tokens * width,
    )[0]


def out_backward(params, incoming, residual, own, other, branch, vectors, scal, pieces):
    rows, count = params
    tokens, width = incoming.shape
    inner = 2 * GROUP

    def body(scal, incoming, residual, own, other, branch, vectors, *rest):
        pieces = rest[: 2 * count]
        residual_grad, branch_grad, keep, send, sums, full, sems = rest[2 * count :]
        copies = start_all(out_pairs(scal, pieces, full, rows, count), sems)
        sums[...] = jnp.zeros_like(sums)

        @pl.loop(0, tokens // ROWS)
        def _(i):
            part = pl.ds(pl.multiple_of(i * ROWS, ROWS), ROWS)
            grad = own[part, :] + other[part, :].astype(F32)
            back, unit = norm_back(residual[part, :], vectors[2:3, :], grad)
            sums[0:1, :] += column_sum(grad * unit)
            sums[1:2, :] += column_sum(grad)
            back = incoming[part, :].astype(F32) + back
            residual_grad[part, :] = back
            sums[2:3, :] += column_sum(back * branch[part, :])
            low = (back * vectors[1:2, :]).astype(BF16)
            branch_grad[part, :] = low
            sums[3:4, :] += column_sum(low.astype(F32))

        wait_all(copies)
        for target, group in ((send, 1 - scal[1]), (keep, scal[1])):
            part = pl.ds(pl.multiple_of(group * GROUP, GROUP), GROUP)
            target[...] = dot_nt(branch_grad[...], full[part, :]).astype(BF16)

    return run_kernel(
        body,
        "out_backward",
        [(scal, "s"), (incoming, "v"), (residual, "v"), (own, "v"), (other, "v"), (branch, "v")]
        + [(vectors, "v")]
        + [(p, "a") for p in pieces],
        [
            ((tokens, width), F32, "v"),
            ((tokens, width), BF16, "v"),
            ((tokens, GROUP), BF16, "v"),
            ((tokens, GROUP), BF16, "v"),
            ((8, width), F32, "v"),
        ],
        [pltpu.VMEM((inner, width), BF16), pltpu.SemaphoreType.DMA((4 * count,))],
        2 * tokens * inner * width,
    )


def attend_backward(keep, other, grad_keep, grad_other, peaks, scal):
    tokens = keep.shape[0]
    total = 2 * tokens
    heads = GROUP // HEAD_DIM

    def body(scal, keep, other, grad_keep, grad_other, peaks, out_keep, out_send, *rest):
        full, grads, out, key_sum, value_sum, sems = rest
        copies = place_tokens(scal, keep, other, full, sems)
        copies += place_tokens(scal, grad_keep, grad_other, grads, sems, 2)
        wait_all(copies)
        length = scal[2]
        for pair in range(heads // 2):
            key_sum[...] = jnp.zeros_like(key_sum)
            value_sum[...] = jnp.zeros_like(value_sum)

            @pl.loop(0, total // CHUNK)
            def _(i):
                part = pl.ds(pl.multiple_of(i * CHUNK, CHUNK), CHUNK)
                query_parts = []
                for side, head in enumerate((2 * pair, 2 * pair + 1)):
                    at = head * HEAD_DIM
                    query = full[part, at : at + HEAD_DIM] * jnp.asarray(HEAD_DIM**-0.5, BF16)
                    key = full[:, GROUP + at : GROUP + at + HEAD_DIM]
                    value = full[:, 2 * GROUP + at : 2 * GROUP + at + HEAD_DIM]
                    grad = grads[part, at : at + HEAD_DIM]
                    low, high = masked(dot_nt(key, query), length)
                    peak = peaks[head : head + 1, part]
                    probs = jnp.concatenate([jnp.exp(low - peak), jnp.exp(high - peak)], axis=0)
                    prob_grad = dot_nt(value, grad)
                    mean = column_sum(probs * prob_grad)
                    score_grad = (probs * (prob_grad - mean)).astype(BF16)
                    lanes = slice(side * HEAD_DIM, (side + 1) * HEAD_DIM)
                    value_sum[:, lanes] += dot_nn(probs.astype(BF16), grad)
                    key_sum[:, lanes] += dot_nn(score_grad, query)
                    query_parts.append(dot_tn(key, score_grad) * HEAD_DIM**-0.5)
                made = jnp.concatenate(query_parts, axis=0)
                out[part, pair * 128 : (pair + 1) * 128] = made.T.astype(BF16)

            at = pair * 128
            out[:, GROUP + at : GROUP + at + 128] = key_sum[...].astype(BF16)
            out[:, 2 * GROUP + at : 2 * GROUP + at + 128] = value_sum[...].astype(BF16)

        split_tokens(scal, out, out_keep, out_send, sems)

    return run_kernel(
        body,
        "attend_backward",
        [(scal, "s"), (keep, "a"), (other, "a"), (grad_keep, "a"), (grad_other, "a")]
        + [(peaks, "v")],
        [((tokens, 3 * GROUP), BF16, "a"), ((tokens, 3 * GROUP), BF16, "a")],
        [
            pltpu.VMEM((total, 3 * GROUP), BF16),
            pltpu.VMEM((total, GROUP), BF16),
            pltpu.VMEM((total, 3 * GROUP), BF16),
            pltpu.VMEM((total, 128), F32),
            pltpu.VMEM((total, 128), F32),
            pltpu.SemaphoreType.DMA((4,)),
        ],
        heads * total * total * HEAD_DIM * 10,
        heads * total * total,
    )


def mix_backward(params, keep, other, scal, pieces, width):
    rows, count = params
    tokens = keep.shape[0]
    inner = 6 * GROUP

    def body(scal, keep, other, *rest):
        pieces = rest[: 2 * count]
        triple, own, send, full, sems = rest[2 * count :]
        copies = place_groups(scal, keep, other, triple, sems)
        copies += start_all(mix_pairs(scal, pieces, full, rows, count), sems, 2)
        wait_all(copies)

        @pl.loop(0, width // GROUP)
        def _(i):
            columns = pl.ds(pl.multiple_of(i * GROUP, GROUP), GROUP)
            made = dot_nt(triple[...], full[columns, :])
            own[:, columns] = made
            send[:, columns] = made.astype(BF16)

    return run_kernel(
        body,
        "mix_backward",
        [(scal, "s"), (keep, "a"), (other, "a")] + [(p, "a") for p in pieces],
        [((tokens, inner), BF16, "v"), ((tokens, width), F32, "v"), ((tokens, width), BF16, "v")],
        [pltpu.VMEM((width, inner), BF16), pltpu.SemaphoreType.DMA((6 * count + 2,))],
        2 * tokens * inner * width,
    )


def mix_weights(params, normed, triple, mixed, branch_grad, scal):
    rows, count = params
    tokens, width = normed.shape
    inner = triple.shape[1]

    def body(scal, normed, triple, mixed, branch_grad, *rest):
        pieces, (sums, full, out, sems) = rest[: 2 * count], rest[2 * count :]
        out[...] = dot_tn(mixed[...], branch_grad[...]).astype(BF16)
        pairs = [(b, a) for a, b in out_pairs(scal, pieces, out, rows, count)]
        copies = start_all(pairs, sems)

        @pl.loop(0, inner // GROUP)
        def _(i):
            part = pl.ds(pl.multiple_of(i * GROUP, GROUP), GROUP)
            full[:, part] = dot_tn(normed[...], triple[:, part]).astype(BF16)
            sums[:, part] = column_sum(triple[:, part].astype(F32))

        pairs = [(b, a) for a, b in mix_pairs(scal, pieces, full, rows, count)]
        wait_all(copies + start_all(pairs, sems, 4 * count))

    return run_kernel(
        body,
        "mix_weights",
        [(scal, "s"), (normed, "v"), (triple, "v"), (mixed, "v"), (branch_grad, "v")],
        [((4 * rows, GROUP), BF16, "a")] * (2 * count) + [((1, inner), F32, "v")],
        [
            pltpu.VMEM((width, inner), BF16),
            pltpu.VMEM((2 * GROUP, width), BF16),
            pltpu.SemaphoreType.DMA((10 * count,)),
        ],
        2 * tokens * width * (inner + 2 * GROUP),
    )


def input_backward(hidden, own, other, residual_grad, gain):
    tokens, width = hidden.shape

    def body(hidden, own, other, residual_grad, gain, input_grad, low_grad, sums):
        sums[...] = jnp.zeros_like(sums)

        @pl.loop(0, tokens // ROWS)
        def _(i):
            part = pl.ds(pl.multiple_of(i * ROWS, ROWS), ROWS)
            grad = own[part, :] + other[part, :].astype(F32)
            back, unit = norm_back(hidden[part, :].astype(F32), gain[...], grad)
            sums[0:1, :] += column_sum(grad * unit)
            sums[1:2, :] += column_sum(grad)
            back = residual_grad[part, :] + back
            input_grad[part, :] = back
            low_grad[part, :] = back.astype(BF16)

    return run_kernel(
        body,
        "input_backward",
        [(hidden, "v"), (own, "v"), (other, "v"), (residual_grad, "v"), (gain, "v")],
        [((tokens, width), F32, "v"), ((tokens, width), BF16, "v"), ((8, width), F32, "v")],
        [],
        20 * tokens * width,
    )


def swap(value, axis, bit):
    count = lax.axis_size(axis)
    return lax.ppermute(value, axis, [(i, i ^ bit) for i in range(count)])


def add_low(left, right):
    return (left.astype(F32) + right.astype(F32)).astype(BF16)


def gather_blocks(halves, bits):
    places = [1 << i for i in range(len(bits))]
    held = {}
    for h, value in enumerate(halves):
        order = list(zip(bits, places))
        order = order if h == 0 else order[::-1]
        blocks = {0: value}
        for bit, place in order:
            for k in list(blocks):
                blocks[k ^ place] = swap(blocks[k], "fsdp", bit)
        for k in blocks:
            held[k, h] = blocks[k]
    return [held[k, h] for k in range(1 << len(bits)) for h in range(2)]


def scatter_blocks(pieces, bits):
    places = [1 << i for i in range(len(bits))]
    results = []
    for h in range(2):
        blocks = {k: pieces[2 * k + h] for k in range(1 << len(bits))}
        order = list(zip(bits, places))
        order = order if h == 0 else order[::-1]
        for bit, place in order:
            for k in [k for k in blocks if k & place]:
                blocks[k ^ place] = add_low(blocks[k ^ place], swap(blocks.pop(k), "fsdp", bit))
        results.append(blocks[0])
    return results


def sum_line(value):
    place = lax.axis_index("seq")
    near = add_low(value, lax.ppermute(value, "seq", [(0, 1), (3, 2)]))
    both = add_low(near, lax.ppermute(near, "seq", [(1, 2), (2, 1)]))
    back = lax.ppermute(both, "seq", [(1, 0), (2, 3)])
    return jnp.where((place == 1) | (place == 2), both, back)


def pick(flag, first, second):
    return jnp.where(flag, first, second)


def pack_mix(mix, out, side, count):
    rows, width = mix.shape[0], out.shape[1]
    split = mix.reshape(rows, 3, count, 2, width // (2 * count))[:, :, :, side]
    split = split.reshape(rows, 3, width // 2)
    half = out[side * rows // 2 : (side + 1) * rows // 2]
    return [
        jnp.concatenate(
            [split[:, t, h * GROUP : (h + 1) * GROUP] for t in range(3)]
            + [half[:, (2 * h + j) * GROUP : (2 * h + j + 1) * GROUP] for j in range(2)],
            axis=0,
        )
        for h in range(2)
    ]


def unpack_mix(sides, count):
    rows = sides[0][0].shape[0] // 4
    width = 4 * GROUP
    mixes, outs = [], []
    for halves in sides:
        parts = [
            jnp.concatenate([halves[h][t * rows : (t + 1) * rows] for h in range(2)], axis=1)
            for t in range(3)
        ]
        mixes.append(jnp.stack(parts, axis=1).reshape(rows, 3, count, width // (2 * count)))
        half = rows // 2
        outs.append(
            jnp.concatenate(
                [
                    halves[h][3 * rows + j * half : 3 * rows + (j + 1) * half]
                    for h in range(2)
                    for j in range(2)
                ],
                axis=1,
            )
        )
    return jnp.stack(mixes, axis=3).reshape(rows, 3 * width), jnp.concatenate(outs, axis=0)


def pack_feed(up, down, side, count):
    rows, inner = up.shape
    split = up.reshape(rows, count, 2, inner // (2 * count))[:, :, side].reshape(rows, inner // 2)
    half = down[side * 2 * rows : (side + 1) * 2 * rows]
    wide, narrow = inner // 8, down.shape[1] // 2
    return [
        jnp.concatenate(
            [split[:, (2 * h + j) * wide : (2 * h + j + 1) * wide] for j in range(2)]
            + [half[:, h * narrow : (h + 1) * narrow]],
            axis=0,
        )
        for h in range(2)
    ]


def unpack_feed(sides, count):
    rows = sides[0][0].shape[0] // 4
    ups, downs = [], []
    for halves in sides:
        up = jnp.concatenate(
            [halves[h][j * rows : (j + 1) * rows] for h in range(2) for j in range(2)], axis=1
        )
        ups.append(up.reshape(rows, count, up.shape[1] // count))
        downs.append(jnp.concatenate([halves[h][2 * rows :] for h in range(2)], axis=1))
    up = jnp.stack(ups, axis=2)
    return up.reshape(rows, -1), jnp.concatenate(downs, axis=0)


def body(activations, cotangent, lengths, *weights):
    mixgain, mixshift, mixweight, mixbias, outweight, outbias, mixscale = weights[:7]
    feedgain, feedshift, upweight, upbias, downweight, downbias, feedscale = weights[7:]
    core, line, spot = (lax.axis_index(a) for a in ("section", "seq", "fsdp"))
    first = core == 0
    parity, micro = line % 2, line // 2
    shards = lax.axis_size("fsdp")
    width = activations.shape[-1]
    inner = upbias.shape[1] * shards
    base_rows = width // shards

    joined, rows = 0, base_rows
    while rows // 2 < HEAD_DIM:
        joined, rows = joined + 1, rows * 2
    count = shards >> joined
    bits = [1 << (joined + i) for i in range(count.bit_length() - 1)]
    params = (rows, count)
    block = spot >> joined

    def join(value):
        for i in range(joined):
            far = swap(value, "fsdp", 1 << i)
            upper = ((spot >> i) & 1) == 1
            value = jnp.concatenate(
                [pick(upper, far, value), pick(upper, value, far)], axis=0
            )
        return value

    def unjoin(value):
        for i in reversed(range(joined)):
            half = value.shape[0] // 2
            upper = ((spot >> i) & 1) == 1
            low, high = value[:half], value[half:]
            value = add_low(pick(upper, high, low), swap(pick(upper, low, high), "fsdp", 1 << i))
        return value

    def spread(packs):
        sides = [packs(0), packs(1)]
        layers = [[], []]
        for h in range(2):
            keep = pick(first, sides[0][h], sides[1][h])
            far = swap(pick(first, sides[1][h], sides[0][h]), "section", 1)
            layers[0].append(pick(first, keep, far))
            layers[1].append(pick(first, far, keep))
        return layers

    mix_shard, out_shard = join(mixweight[0]), join(outweight[0])
    up_shard, down_shard = join(upweight[0]), join(downweight[0])
    mix_halves = spread(lambda side: pack_mix(mix_shard, out_shard, side, count))
    feed_halves = spread(lambda side: pack_feed(up_shard, down_shard, side, count))
    mix_pieces, feed_pieces = [], []
    for layer in range(2):
        mix_pieces.append(gather_blocks(mix_halves[layer], bits))
        feed_pieces.append(gather_blocks(feed_halves[layer], bits))

    packed = jnp.concatenate(
        [mixgain[0], mixshift[0], mixbias[0, 0], mixbias[0, 1], outbias[0], mixscale[0]]
        + [feedgain[0], feedshift[0], downbias[0], feedscale[0], upbias[0]]
    )
    packed = lax.all_gather(packed, ("section", "fsdp"), axis=0)
    packed = packed.reshape(2, shards, -1).astype(F32)

    def vector(layer, index):
        taken = packed[layer, :, index * base_rows : (index + 1) * base_rows]
        return taken.reshape(1, width)

    def half_vector(value):
        value = value.reshape(count, 2, -1)
        return pick(first, value[:, 0], value[:, 1]).reshape(1, -1)

    def mix_bias(layer):
        query = half_vector(vector(layer, 2)).reshape(2, 1, GROUP)
        value = half_vector(vector(layer, 3)).reshape(2, 1, GROUP)
        return jnp.concatenate([query, jnp.zeros_like(query), value], axis=1).reshape(1, -1)

    low_micro = micro == 0
    tokens = activations.shape[2]

    def to_pair(value):
        keep = pick(low_micro, value[0, 0], value[1, 0])
        far = swap(pick(low_micro, value[1, 0], value[0, 0]), "seq", 2)
        return jnp.concatenate([pick(low_micro, keep, far), pick(low_micro, far, keep)], axis=0)

    def from_pair(value):
        low, high = value[:tokens], value[tokens:]
        far = swap(pick(low_micro, high, low).astype(BF16), "seq", 2).astype(value.dtype)
        keep = pick(low_micro, low, high)
        return jnp.stack([pick(low_micro, keep, far), pick(low_micro, far, keep)])[None, :, None]

    length = pick(low_micro, lengths[0, 0], lengths[1, 0])
    scal = jnp.stack([block, parity, length]).astype(jnp.int32)

    hidden = to_pair(activations)
    incoming = to_pair(cotangent)
    kept, results = [], []
    for layer in range(2):
        pieces, feeds = mix_pieces[layer], feed_pieces[layer]
        normed, keep, send = mix_forward(
            params, hidden, vector(layer, 0), vector(layer, 1), mix_bias(layer), scal, pieces
        )
        other = swap(send, "seq", 1)
        out_keep, out_send, peaks = attend_forward(keep, other, scal)
        out_other = swap(out_send, "seq", 1)
        mixed, own, send = out_forward(params, out_keep, out_other, scal, pieces, width)
        far = swap(send, "section", 1)
        vectors = jnp.concatenate([vector(layer, i) for i in (4, 5, 6, 7)], axis=0)
        up_bias = half_vector(packed[layer, :, 10 * base_rows :].reshape(1, inner))
        branch, residual, normed_two, active, slope, own, send = feed_forward(
            params, hidden, own, far, vectors, up_bias, scal, feeds
        )
        far = swap(send, "section", 1)
        kept.append(
            (hidden, normed, keep, other, peaks, mixed, branch, residual, normed_two, active)
            + (slope, own, far, vectors)
        )
        made = own + far.astype(F32) + vector(layer, 8)
        hidden = (residual + vector(layer, 9) * made).astype(BF16)
        results.append(hidden)

    gradients, sums, mix_shares, feed_shares = [None] * 2, [None] * 2, [None] * 2, [None] * 2
    for layer in (1, 0):
        pieces, feeds = mix_pieces[layer], feed_pieces[layer]
        hidden, normed, keep, other, peaks, mixed, branch, residual, normed_two, active = kept[
            layer
        ][:10]
        slope, branch_own, branch_far, vectors = kept[layer][10:]
        lower, up_grad, up_sum, own, send = feed_backward(
            params, incoming, vector(layer, 9), slope, scal, feeds
        )
        far = swap(send, "section", 1)
        grads = feed_weights(params, active, lower, normed_two, up_grad, scal)
        feed_shares[layer] = [sum_line(v) for v in scatter_blocks(grads, bits)]
        feed_sum = feed_sums(incoming, branch_own, branch_far, vector(layer, 8), lower)
        residual_grad, branch_grad, grad_keep, grad_send, out_sum = out_backward(
            params, incoming, residual, own, far, branch, vectors, scal, pieces
        )
        grad_other = swap(grad_send, "seq", 1)
        triple_keep, triple_send = attend_backward(
            keep, other, grad_keep, grad_other, peaks, scal
        )
        triple_other = swap(triple_send, "seq", 1)
        triple, own, send = mix_backward(params, triple_keep, triple_other, scal, pieces, width)
        far = swap(send, "section", 1)
        *grads, mix_sum = mix_weights(params, normed, triple, mixed, branch_grad, scal)
        mix_shares[layer] = [sum_line(v) for v in scatter_blocks(grads, bits)]
        input_grad, incoming, in_sum = input_backward(
            hidden, own, far, residual_grad, vector(layer, 0)
        )
        gradients[layer] = input_grad
        mix_sum = mix_sum.reshape(2, 3, GROUP)
        sums[layer] = (
            jnp.concatenate([in_sum[:2], out_sum[:4], feed_sum[:2]], axis=0).reshape(-1),
            jnp.concatenate([up_sum.reshape(-1), mix_sum[:, 0].reshape(-1), mix_sum[:, 2].reshape(-1)]),
        )

    whole = pick(first, sums[0][0], sums[1][0])
    own_half = pick(first, sums[0][1], sums[1][1])
    far_half = swap(pick(first, sums[1][1], sums[0][1]), "section", 1)
    totals = jnp.concatenate(
        [whole, pick(first, own_half, far_half), pick(first, far_half, own_half)]
    ).reshape(-1, 128)
    for axis in ("fsdp", "seq"):
        bit = 1
        while bit < lax.axis_size(axis):
            totals = totals + swap(totals, axis, bit)
            bit *= 2
    totals = totals.reshape(-1)
    whole = totals[: 8 * width].reshape(8, width)
    halves = totals[8 * width :].reshape(2, -1)
    half = inner // 2
    up_total = jnp.stack([halves[s, :half].reshape(count, -1) for s in range(2)], axis=1)
    bias_total = jnp.stack(
        [halves[s, half:].reshape(2, count, -1) for s in range(2)], axis=2
    ).reshape(2, width)

    def own_part(value, size):
        return lax.dynamic_slice_in_dim(value, spot * size, size, axis=value.ndim - 1)

    whole = own_part(whole, base_rows)[:, None]
    up_total = own_part(up_total.reshape(inner), inner // shards)[None]
    bias_total = own_part(bias_total, base_rows)[None]

    def collect(shares):
        sides = [[], []]
        for h in range(2):
            early = lax.ppermute(shares[1][h], "section", [(0, 1)])
            late = lax.ppermute(shares[0][h], "section", [(1, 0)])
            sides[0].append(pick(first, shares[0][h], early))
            sides[1].append(pick(first, late, shares[1][h]))
        return sides

    mix_total, out_total = unpack_mix(collect(mix_shares), count)
    up_weight, down_weight = unpack_feed(collect(feed_shares), count)

    def final(value):
        return unjoin(value).astype(F32)[None]

    return (
        from_pair(pick(first, results[0], results[1])),
        from_pair(pick(first, gradients[0], gradients[1])),
        whole[0],
        whole[1],
        final(mix_total),
        bias_total,
        final(out_total),
        whole[5],
        whole[4],
        whole[2],
        whole[3],
        final(up_weight),
        up_total,
        final(down_weight),
        whole[7],
        whole[6],
    )


def solution(mesh):
    rowed, flat = P("section", "fsdp", None), P("section", "fsdp")
    image = P(None, "fsdp", "seq", None)
    bias = P("section", None, "fsdp")
    kept = P("section", None, "fsdp", "seq", None)
    params = (flat, flat, rowed, bias, rowed, flat, flat, flat, flat, rowed, flat, rowed, flat, flat)
    return jax.shard_map(
        body,
        mesh=mesh,
        in_specs=(image, image, P(None, "fsdp")) + params,
        out_specs=(kept, kept) + params,
        check_vma=False,
    )
```

```python
import math

import jax
import jax.numpy as jnp
from jax import lax
from jax.experimental import pallas as pl
from jax.experimental.pallas import tpu as pltpu
from jax.sharding import PartitionSpec as P

HEAD_DIM = 64
EPSILON = 1e-06
NEGATIVE = -1000000000.0
F32 = jnp.float32
BF16 = jnp.bfloat16
GROUP = 256
MIN_LENGTH = 896
CHUNK = 256
ROWS = 64
MIB = 1024 * 1024


def dot_nn(left, right):
    return lax.dot_general(left, right, (((1,), (0,)), ((), ())), preferred_element_type=F32)


def dot_nt(left, right):
    return lax.dot_general(left, right, (((1,), (1,)), ((), ())), preferred_element_type=F32)


def dot_tn(left, right):
    return lax.dot_general(left, right, (((0,), (0,)), ((), ())), preferred_element_type=F32)


def size_of(shape, dtype):
    return math.prod(shape) * jnp.dtype(dtype).itemsize


def run_kernel(kernel, name, ins, outs, scratch, flops, exps=0, deps=()):
    deps = list(deps)

    def body(*refs):
        kernel(*refs[len(deps) :])

    spaces = {"v": pltpu.VMEM, "a": pl.ANY, "s": pltpu.SMEM}
    moved = sum(size_of(a.shape, a.dtype) for a, _ in ins) + sum(size_of(s, d) for s, d, _ in outs)
    held = sum(size_of(a.shape, a.dtype) for a, k in ins if k == "v")
    ins = [(a, "a") for a in deps] + ins
    held += sum(size_of(s, d) for s, d, k in outs if k == "v")
    held += sum(size_of(s.shape, s.dtype) for s in scratch if s.memory_space == pltpu.VMEM)
    return pl.pallas_call(
        body,
        name=name,
        out_shape=[jax.ShapeDtypeStruct(s, d) for s, d, _ in outs],
        in_specs=[pl.BlockSpec(memory_space=spaces[k]) for _, k in ins],
        out_specs=[pl.BlockSpec(memory_space=spaces[k]) for _, _, k in outs],
        scratch_shapes=scratch,
        compiler_params=pltpu.CompilerParams(vmem_limit_bytes=min(held + 14 * MIB, 58 * MIB)),
        cost_estimate=pl.CostEstimate(flops=flops, bytes_accessed=moved, transcendentals=exps),
    )(*[a for a, _ in ins])


def start_all(pairs, sems, first=0):
    copies = []
    for index, (source, target) in enumerate(pairs):
        copies.append(pltpu.make_async_copy(source, target, sems.at[first + index]))
        copies[-1].start()
    return copies


def wait_all(copies):
    for copy in copies:
        copy.wait()


def block_rows(scal, k, rows):
    return pl.ds(pl.multiple_of((scal[0] ^ k) * rows, rows), rows)


def scatter_groups(count, h):
    places = [1 << i for i in range(count.bit_length() - 1)]
    groups = [[0]]
    for place in places[::-1] if h == 0 else places:
        groups.insert(0, [k ^ place for group in groups for k in group])
    return groups


def group_shapes(shape, count):
    return [
        ((len(group) * shape[0], shape[1]), BF16, "a")
        for h in range(2)
        for group in scatter_groups(count, h)
    ]


def group_views(refs, size, count):
    views, refs = {}, list(refs)
    for h in range(2):
        for group in scatter_groups(count, h):
            ref = refs.pop(0)
            for place, k in enumerate(group):
                views[2 * k + h] = ref.at[place * size : (place + 1) * size, :]
    return [views[i] for i in range(2 * count)]


def mix_pairs(scal, pieces, full, rows, count):
    return [
        (
            pieces[2 * k + h].at[t * rows : (t + 1) * rows, :],
            full.at[block_rows(scal, k, rows), (3 * h + t) * GROUP : (3 * h + t + 1) * GROUP],
        )
        for k in range(count)
        for h in range(2)
        for t in range(3)
    ]


def out_pairs(scal, pieces, full, rows, count):
    half = rows // 2
    return [
        (
            pieces[2 * k + h].at[3 * rows + j * half : 3 * rows + (j + 1) * half, :],
            full.at[block_rows(scal, k, half), (2 * h + j) * GROUP : (2 * h + j + 1) * GROUP],
        )
        for k in range(count)
        for h in range(2)
        for j in range(2)
    ]


def up_pairs(scal, pieces, full, rows, count):
    width = pieces[0].shape[1]
    return [
        (
            pieces[2 * k + h].at[j * rows : (j + 1) * rows, :],
            full.at[block_rows(scal, k, rows), (2 * h + j) * width : (2 * h + j + 1) * width],
        )
        for k in range(count)
        for h in range(2)
        for j in range(2)
    ]


def down_pairs(scal, pieces, full, rows, count):
    width = pieces[0].shape[1]
    return [
        (
            pieces[2 * k + h].at[2 * rows : 4 * rows, :],
            full.at[block_rows(scal, k, 2 * rows), h * width : (h + 1) * width],
        )
        for k in range(count)
        for h in range(2)
    ]


def norm_parts(values):
    center = jnp.mean(values, axis=-1, keepdims=True)
    centered = values - center
    spread = jnp.mean(centered * centered, axis=-1, keepdims=True)
    inverse = lax.rsqrt(spread + EPSILON)
    return centered * inverse, inverse


def norm_back(values, gain, grad):
    unit, inverse = norm_parts(values)
    scaled = grad * gain
    mean_one = jnp.mean(scaled, axis=-1, keepdims=True)
    mean_two = jnp.mean(scaled * unit, axis=-1, keepdims=True)
    return inverse * (scaled - mean_one - unit * mean_two), unit


def column_sum(values):
    return jnp.sum(values, axis=0, keepdims=True)


def gelu_pair(values):
    energy = jnp.exp(values * values * -0.5)
    t = 1.0 / (1.0 + (0.3275911 * 0.7071067811865476) * jnp.abs(values))
    tail = 1.061405429 * 0.5
    for factor in (-1.453152027, 1.421413741, -0.284496736, 0.254829592):
        tail = tail * t + factor * 0.5
    tail = tail * t * energy
    below = jnp.where(values >= 0, 1.0 - tail, tail)
    return values * below, below + values * energy * 0.3989422804014327


def mix_forward(params, hidden, vectors, bias, scal, pieces, deps):
    rows, count = params
    tokens, width = hidden.shape
    span = 3 * GROUP

    def body(scal, hidden, vectors, bias, *rest):
        pieces, (normed, keep, send, full, sems) = rest[: 2 * count], rest[2 * count :]
        copies = start_all(mix_pairs(scal, pieces, full, rows, count), sems)

        @pl.loop(0, tokens // ROWS)
        def _(i):
            part = pl.ds(pl.multiple_of(i * ROWS, ROWS), ROWS)
            unit, _ = norm_parts(hidden[part, :].astype(F32))
            normed[part, :] = (unit * vectors[0:1, :] + vectors[1:2, :]).astype(BF16)

        wait_all(copies)
        for target, group in ((send, 1 - scal[1]), (keep, scal[1])):
            for t in range(3):
                columns = pl.ds(pl.multiple_of((group * 3 + t) * GROUP, GROUP), GROUP)
                made = dot_nn(normed[...], full[:, columns]) + bias[:, columns]
                target[:, t * GROUP : (t + 1) * GROUP] = made.astype(BF16)

    return run_kernel(
        body,
        "mix_forward",
        [(scal, "s"), (hidden, "v"), (vectors, "v"), (bias, "v")] + [(p, "a") for p in pieces],
        [((tokens, width), BF16, "v"), ((tokens, span), BF16, "v"), ((tokens, span), BF16, "v")],
        [pltpu.VMEM((width, 2 * span), BF16), pltpu.SemaphoreType.DMA((6 * count,))],
        4 * tokens * width * span,
        deps=deps,
    )


def place_tokens(scal, keep, other, full, sems, first=0):
    tokens = keep.shape[0]
    own = pl.ds(pl.multiple_of(scal[1] * tokens, tokens), tokens)
    far = pl.ds(pl.multiple_of((1 - scal[1]) * tokens, tokens), tokens)
    return start_all([(keep, full.at[own, :]), (other, full.at[far, :])], sems, first)


def split_tokens(scal, full, keep, send, sems):
    tokens = keep.shape[0]
    own = pl.ds(pl.multiple_of(scal[1] * tokens, tokens), tokens)
    far = pl.ds(pl.multiple_of((1 - scal[1]) * tokens, tokens), tokens)
    wait_all(start_all([(full.at[far, :], send), (full.at[own, :], keep)], sems))


def masked(scores, length):
    start = MIN_LENGTH
    tail = scores[start:, :]
    position = lax.broadcasted_iota(jnp.int32, tail.shape, 0) + start
    return scores[:start, :], jnp.where(position < length, tail, NEGATIVE)


def attend_forward(keep, other, scal, deps):
    tokens = keep.shape[0]
    total = 2 * tokens
    heads = GROUP // HEAD_DIM

    def body(scal, keep, other, out_keep, out_send, peaks, full, out, sems):
        wait_all(place_tokens(scal, keep, other, full, sems))
        length = scal[2]
        for pair in range(heads // 2):

            @pl.loop(0, total // CHUNK)
            def _(i):
                part = pl.ds(pl.multiple_of(i * CHUNK, CHUNK), CHUNK)
                outs = []
                for head in (2 * pair, 2 * pair + 1):
                    at = head * HEAD_DIM
                    query = full[part, at : at + HEAD_DIM] * jnp.asarray(HEAD_DIM**-0.5, BF16)
                    key = full[:, GROUP + at : GROUP + at + HEAD_DIM]
                    value = full[:, 2 * GROUP + at : 2 * GROUP + at + HEAD_DIM]
                    low, high = masked(dot_nt(key, query), length)
                    peak = jnp.maximum(
                        jnp.max(low, axis=0, keepdims=True), jnp.max(high, axis=0, keepdims=True)
                    )
                    low = jnp.exp(low - peak)
                    high = jnp.exp(high - peak)
                    mass = column_sum(low) + column_sum(high)
                    probs = jnp.concatenate([low.astype(BF16), high.astype(BF16)], axis=0)
                    outs.append(dot_tn(value, probs) / mass)
                    peaks[head : head + 1, part] = peak + jnp.log(mass)
                made = jnp.concatenate(outs, axis=0)
                out[part, pair * 128 : (pair + 1) * 128] = made.T.astype(BF16)

        split_tokens(scal, out, out_keep, out_send, sems)

    return run_kernel(
        body,
        "attend_forward",
        [(scal, "s"), (keep, "a"), (other, "a")],
        [
            ((tokens, GROUP), BF16, "a"),
            ((tokens, GROUP), BF16, "a"),
            ((8, total), F32, "v"),
        ],
        [
            pltpu.VMEM((total, 3 * GROUP), BF16),
            pltpu.VMEM((total, GROUP), BF16),
            pltpu.SemaphoreType.DMA((2,)),
        ],
        heads * total * total * HEAD_DIM * 4,
        heads * total * total,
        deps,
    )


def place_groups(scal, keep, other, full, sems, first=0):
    width = keep.shape[1]
    own = pl.ds(pl.multiple_of(scal[1] * width, width), width)
    far = pl.ds(pl.multiple_of((1 - scal[1]) * width, width), width)
    return start_all([(keep, full.at[:, own]), (other, full.at[:, far])], sems, first)


def out_forward(params, keep, other, scal, pieces, width, deps):
    rows, count = params
    tokens = keep.shape[0]
    inner = 2 * GROUP

    def body(scal, keep, other, *rest):
        pieces, (mixed, own, send, full, sems) = rest[: 2 * count], rest[2 * count :]
        copies = place_groups(scal, keep, other, mixed, sems)
        copies += start_all(out_pairs(scal, pieces, full, rows, count), sems, 2)
        wait_all(copies)
        for j in range(width // GROUP):
            columns = slice(j * GROUP, (j + 1) * GROUP)
            made = dot_nn(mixed[...], full[:, columns])
            own[:, columns] = made
            send[:, columns] = made.astype(BF16)

    return run_kernel(
        body,
        "out_forward",
        [(scal, "s"), (keep, "a"), (other, "a")] + [(p, "a") for p in pieces],
        [((tokens, inner), BF16, "v"), ((tokens, width), F32, "v"), ((tokens, width), BF16, "v")],
        [pltpu.VMEM((inner, width), BF16), pltpu.SemaphoreType.DMA((4 * count + 2,))],
        2 * tokens * inner * width,
        deps=deps,
    )


def feed_forward(params, hidden, own, other, vectors, upbias, scal, pieces, deps):
    rows, count = params
    tokens, width = hidden.shape
    inner = upbias.shape[1]
    tile = 512

    def body(scal, hidden, own, other, vectors, upbias, *rest):
        pieces = rest[: 2 * count]
        branch, residual, normed, active, slope, made_own, made_send, up, down, sems = rest[
            2 * count :
        ]
        up_copies = start_all(up_pairs(scal, pieces, up, rows, count), sems)
        down_copies = start_all(down_pairs(scal, pieces, down, rows, count), sems, 4 * count)

        @pl.loop(0, tokens // ROWS)
        def _(i):
            part = pl.ds(pl.multiple_of(i * ROWS, ROWS), ROWS)
            made = own[part, :] + other[part, :].astype(F32) + vectors[4:5, :]
            branch[part, :] = made
            made = hidden[part, :].astype(F32) + vectors[5:6, :] * made
            residual[part, :] = made
            unit, _ = norm_parts(made)
            normed[part, :] = (unit * vectors[6:7, :] + vectors[7:8, :]).astype(BF16)

        wait_all(up_copies)

        @pl.loop(0, inner // tile)
        def _(i):
            columns = pl.ds(pl.multiple_of(i * tile, tile), tile)
            for r in range(tokens // 256):
                part = slice(r * 256, (r + 1) * 256)
                made = dot_nn(normed[part, :], up[:, columns]) + upbias[:, columns]
                value, gradient = gelu_pair(made)
                active[part, columns] = value.astype(BF16)
                slope[part, columns] = gradient.astype(BF16)

        wait_all(down_copies)

        @pl.loop(0, width // GROUP)
        def _(i):
            columns = pl.ds(pl.multiple_of(i * GROUP, GROUP), GROUP)
            made = dot_nn(active[...], down[:, columns])
            made_own[:, columns] = made
            made_send[:, columns] = made.astype(BF16)

    return run_kernel(
        body,
        "feed_forward",
        [(scal, "s"), (hidden, "v"), (own, "v"), (other, "v"), (vectors, "v"), (upbias, "v")]
        + [(p, "a") for p in pieces],
        [
            ((tokens, width), F32, "v"),
            ((tokens, width), F32, "v"),
            ((tokens, width), BF16, "v"),
            ((tokens, inner), BF16, "v"),
            ((tokens, inner), BF16, "v"),
            ((tokens, width), F32, "v"),
            ((tokens, width), BF16, "v"),
        ],
        [
            pltpu.VMEM((width, inner), BF16),
            pltpu.VMEM((inner, width), BF16),
            pltpu.SemaphoreType.DMA((6 * count,)),
        ],
        4 * tokens * width * inner,
        2 * tokens * inner,
        deps,
    )


def layer_result(residual, own, other, vectors, deps):
    tokens, width = residual.shape

    def body(residual, own, other, vectors, made):
        @pl.loop(0, tokens // ROWS)
        def _(i):
            part = pl.ds(pl.multiple_of(i * ROWS, ROWS), ROWS)
            branch = own[part, :] + other[part, :].astype(F32) + vectors[8:9, :]
            made[part, :] = (residual[part, :] + vectors[9:10, :] * branch).astype(BF16)

    return run_kernel(
        body,
        "layer_result",
        [(residual, "v"), (own, "v"), (other, "v"), (vectors, "v")],
        [((tokens, width), BF16, "v")],
        [],
        4 * tokens * width,
        deps=deps,
    )[0]


def feed_backward(params, incoming, vectors, slope, scal, pieces, deps):
    rows, count = params
    tokens, width = incoming.shape
    inner = slope.shape[1]
    tile = 512

    def body(scal, incoming, vectors, slope, *rest):
        pieces = rest[: 2 * count]
        lower, up_grad, bias_grad, made_own, made_send, up, down, sems = rest[2 * count :]
        down_copies = start_all(down_pairs(scal, pieces, down, rows, count), sems)
        up_copies = start_all(up_pairs(scal, pieces, up, rows, count), sems, 2 * count)

        @pl.loop(0, tokens // ROWS)
        def _(i):
            part = pl.ds(pl.multiple_of(i * ROWS, ROWS), ROWS)
            lower[part, :] = (incoming[part, :].astype(F32) * vectors[9:10, :]).astype(BF16)

        wait_all(down_copies)

        @pl.loop(0, inner // tile)
        def _(i):
            columns = pl.ds(pl.multiple_of(i * tile, tile), tile)
            made = dot_nt(lower[...], down[columns, :])
            made = (made * slope[:, columns].astype(F32)).astype(BF16)
            up_grad[:, columns] = made
            bias_grad[:, columns] = column_sum(made.astype(F32))

        wait_all(up_copies)

        @pl.loop(0, width // GROUP)
        def _(i):
            columns = pl.ds(pl.multiple_of(i * GROUP, GROUP), GROUP)
            made = dot_nt(up_grad[...], up[columns, :])
            made_own[:, columns] = made
            made_send[:, columns] = made.astype(BF16)

    return run_kernel(
        body,
        "feed_backward",
        [(scal, "s"), (incoming, "v"), (vectors, "v"), (slope, "v")]
        + [(p, "a") for p in pieces],
        [
            ((tokens, width), BF16, "v"),
            ((tokens, inner), BF16, "v"),
            ((1, inner), F32, "v"),
            ((tokens, width), F32, "v"),
            ((tokens, width), BF16, "v"),
        ],
        [
            pltpu.VMEM((width, inner), BF16),
            pltpu.VMEM((inner, width), BF16),
            pltpu.SemaphoreType.DMA((6 * count,)),
        ],
        4 * tokens * width * inner,
        deps=deps,
    )


def feed_weights(params, active, lower, normed, up_grad, scal, deps):
    rows, count = params
    tokens, width = lower.shape
    inner = active.shape[1]
    shape = (4 * rows, inner // 4)
    tile = 512

    def body(scal, active, lower, normed, up_grad, *rest):
        pieces, (up, down, sems) = group_views(rest[:-3], 4 * rows, count), rest[-3:]

        @pl.loop(0, inner // tile)
        def _(i):
            part = pl.ds(pl.multiple_of(i * tile, tile), tile)
            down[part, :] = dot_tn(active[:, part], lower[...]).astype(BF16)

        pairs = [(b, a) for a, b in down_pairs(scal, pieces, down, rows, count)]
        copies = start_all(pairs, sems)

        @pl.loop(0, inner // tile)
        def _(i):
            part = pl.ds(pl.multiple_of(i * tile, tile), tile)
            up[:, part] = dot_tn(normed[...], up_grad[:, part]).astype(BF16)

        pairs = [(b, a) for a, b in up_pairs(scal, pieces, up, rows, count)]
        wait_all(copies + start_all(pairs, sems, 2 * count))

    return run_kernel(
        body,
        "feed_weights",
        [(scal, "s"), (active, "v"), (lower, "v"), (normed, "v"), (up_grad, "v")],
        group_shapes(shape, count),
        [
            pltpu.VMEM((width, inner), BF16),
            pltpu.VMEM((inner, width), BF16),
            pltpu.SemaphoreType.DMA((6 * count,)),
        ],
        4 * tokens * width * inner,
        deps=deps,
    )


def feed_sums(incoming, own, other, vectors, lower):
    tokens, width = incoming.shape

    def body(incoming, own, other, vectors, lower, sums):
        sums[...] = jnp.zeros_like(sums)

        @pl.loop(0, tokens // ROWS)
        def _(i):
            part = pl.ds(pl.multiple_of(i * ROWS, ROWS), ROWS)
            branch = own[part, :] + other[part, :].astype(F32) + vectors[8:9, :]
            sums[0:1, :] += column_sum(branch * incoming[part, :].astype(F32))
            sums[1:2, :] += column_sum(lower[part, :].astype(F32))

    return run_kernel(
        body,
        "feed_sums",
        [(incoming, "v"), (own, "v"), (other, "v"), (vectors, "v"), (lower, "v")],
        [((8, width), F32, "v")],
        [],
        4 * tokens * width,
    )[0]


def out_backward(params, incoming, residual, own, other, branch, vectors, scal, pieces, deps):
    rows, count = params
    tokens, width = incoming.shape
    inner = 2 * GROUP

    def body(scal, incoming, residual, own, other, branch, vectors, *rest):
        pieces = rest[: 2 * count]
        residual_grad, branch_grad, keep, send, sums, full, sems = rest[2 * count :]
        copies = start_all(out_pairs(scal, pieces, full, rows, count), sems)
        sums[...] = jnp.zeros_like(sums)

        @pl.loop(0, tokens // ROWS)
        def _(i):
            part = pl.ds(pl.multiple_of(i * ROWS, ROWS), ROWS)
            grad = own[part, :] + other[part, :].astype(F32)
            back, unit = norm_back(residual[part, :], vectors[6:7, :], grad)
            sums[0:1, :] += column_sum(grad * unit)
            sums[1:2, :] += column_sum(grad)
            back = incoming[part, :].astype(F32) + back
            residual_grad[part, :] = back
            sums[2:3, :] += column_sum(back * branch[part, :])
            low = (back * vectors[5:6, :]).astype(BF16)
            branch_grad[part, :] = low
            sums[3:4, :] += column_sum(low.astype(F32))

        wait_all(copies)
        for target, group in ((send, 1 - scal[1]), (keep, scal[1])):
            part = pl.ds(pl.multiple_of(group * GROUP, GROUP), GROUP)
            target[...] = dot_nt(branch_grad[...], full[part, :]).astype(BF16)

    return run_kernel(
        body,
        "out_backward",
        [(scal, "s"), (incoming, "v"), (residual, "v"), (own, "v"), (other, "v"), (branch, "v")]
        + [(vectors, "v")]
        + [(p, "a") for p in pieces],
        [
            ((tokens, width), F32, "v"),
            ((tokens, width), BF16, "v"),
            ((tokens, GROUP), BF16, "v"),
            ((tokens, GROUP), BF16, "v"),
            ((8, width), F32, "v"),
        ],
        [pltpu.VMEM((inner, width), BF16), pltpu.SemaphoreType.DMA((4 * count,))],
        2 * tokens * inner * width,
        deps=deps,
    )


def attend_backward(keep, other, grad_keep, grad_other, peaks, scal, deps):
    tokens = keep.shape[0]
    total = 2 * tokens
    heads = GROUP // HEAD_DIM

    def body(scal, keep, other, grad_keep, grad_other, peaks, out_keep, out_send, *rest):
        full, grads, out, key_sum, value_sum, sems = rest
        copies = place_tokens(scal, keep, other, full, sems)
        copies += place_tokens(scal, grad_keep, grad_other, grads, sems, 2)
        wait_all(copies)
        length = scal[2]
        for pair in range(heads // 2):
            key_sum[...] = jnp.zeros_like(key_sum)
            value_sum[...] = jnp.zeros_like(value_sum)

            @pl.loop(0, total // CHUNK)
            def _(i):
                part = pl.ds(pl.multiple_of(i * CHUNK, CHUNK), CHUNK)
                query_parts = []
                for side, head in enumerate((2 * pair, 2 * pair + 1)):
                    at = head * HEAD_DIM
                    query = full[part, at : at + HEAD_DIM] * jnp.asarray(HEAD_DIM**-0.5, BF16)
                    key = full[:, GROUP + at : GROUP + at + HEAD_DIM]
                    value = full[:, 2 * GROUP + at : 2 * GROUP + at + HEAD_DIM]
                    grad = grads[part, at : at + HEAD_DIM]
                    low, high = masked(dot_nt(key, query), length)
                    peak = peaks[head : head + 1, part]
                    probs = jnp.concatenate([jnp.exp(low - peak), jnp.exp(high - peak)], axis=0)
                    prob_grad = dot_nt(value, grad)
                    mean = column_sum(probs * prob_grad)
                    score_grad = (probs * (prob_grad - mean)).astype(BF16)
                    lanes = slice(side * HEAD_DIM, (side + 1) * HEAD_DIM)
                    value_sum[:, lanes] += dot_nn(probs.astype(BF16), grad)
                    key_sum[:, lanes] += dot_nn(score_grad, query)
                    query_parts.append(dot_tn(key, score_grad) * HEAD_DIM**-0.5)
                made = jnp.concatenate(query_parts, axis=0)
                out[part, pair * 128 : (pair + 1) * 128] = made.T.astype(BF16)

            at = pair * 128
            out[:, GROUP + at : GROUP + at + 128] = key_sum[...].astype(BF16)
            out[:, 2 * GROUP + at : 2 * GROUP + at + 128] = value_sum[...].astype(BF16)

        split_tokens(scal, out, out_keep, out_send, sems)

    return run_kernel(
        body,
        "attend_backward",
        [(scal, "s"), (keep, "a"), (other, "a"), (grad_keep, "a"), (grad_other, "a")]
        + [(peaks, "v")],
        [((tokens, 3 * GROUP), BF16, "a"), ((tokens, 3 * GROUP), BF16, "a")],
        [
            pltpu.VMEM((total, 3 * GROUP), BF16),
            pltpu.VMEM((total, GROUP), BF16),
            pltpu.VMEM((total, 3 * GROUP), BF16),
            pltpu.VMEM((total, 128), F32),
            pltpu.VMEM((total, 128), F32),
            pltpu.SemaphoreType.DMA((4,)),
        ],
        heads * total * total * HEAD_DIM * 10,
        heads * total * total,
        deps,
    )


def mix_backward(params, keep, other, scal, pieces, width, deps):
    rows, count = params
    tokens = keep.shape[0]
    inner = 6 * GROUP

    def body(scal, keep, other, *rest):
        pieces = rest[: 2 * count]
        triple, own, send, full, sems = rest[2 * count :]
        copies = place_groups(scal, keep, other, triple, sems)
        copies += start_all(mix_pairs(scal, pieces, full, rows, count), sems, 2)
        wait_all(copies)

        @pl.loop(0, width // GROUP)
        def _(i):
            columns = pl.ds(pl.multiple_of(i * GROUP, GROUP), GROUP)
            made = dot_nt(triple[...], full[columns, :])
            own[:, columns] = made
            send[:, columns] = made.astype(BF16)

    return run_kernel(
        body,
        "mix_backward",
        [(scal, "s"), (keep, "a"), (other, "a")] + [(p, "a") for p in pieces],
        [((tokens, inner), BF16, "v"), ((tokens, width), F32, "v"), ((tokens, width), BF16, "v")],
        [pltpu.VMEM((width, inner), BF16), pltpu.SemaphoreType.DMA((6 * count + 2,))],
        2 * tokens * inner * width,
        deps=deps,
    )


def mix_weights(params, normed, triple, mixed, branch_grad, sums, scal, deps):
    rows, count = params
    tokens, width = normed.shape
    inner = triple.shape[1]

    extra, half = 16, rows // 2

    def body(scal, normed, triple, mixed, branch_grad, in_sum, out_sum, feed_sum, up_sum, *rest):
        refs, (full, out, vectors, low, bias, sems) = rest[:-6], rest[-6:]
        pieces = group_views(refs, 4 * rows + extra, count)
        out[...] = dot_tn(mixed[...], branch_grad[...]).astype(BF16)
        pairs = [(b, a) for a, b in out_pairs(scal, pieces, out, rows, count)]
        copies = start_all(pairs, sems)

        @pl.loop(0, inner // GROUP)
        def _(i):
            part = pl.ds(pl.multiple_of(i * GROUP, GROUP), GROUP)
            full[:, part] = dot_tn(normed[...], triple[:, part]).astype(BF16)
            bias[0:1, part] = column_sum(triple[:, part].astype(F32))

        pairs = [(b, a) for a, b in mix_pairs(scal, pieces, full, rows, count)]
        copies += start_all(pairs, sems, 4 * count)
        vectors[...] = jnp.zeros_like(vectors)
        vectors[0:2, :] = in_sum[0:2, :]
        vectors[2:6, :] = out_sum[0:4, :]
        vectors[6:8, :] = feed_sum[0:2, :]
        for j in range(2):
            for b in range(count):
                at = (2 * b + j) * rows
                vectors[8 + j : 9 + j, b * rows : (b + 1) * rows] = up_sum[:, at : at + rows]
        for side, t in enumerate((0, 2)):
            row = jnp.concatenate(
                [bias[0:1, (3 * h + t) * GROUP : (3 * h + t + 1) * GROUP] for h in range(2)], axis=1
            )
            for b in range(count):
                at = b * rows + side * half
                vectors[10:11, at : at + half] = row[:, b * half : (b + 1) * half]
        low[...] = vectors[...].astype(BF16)
        pairs = [
            (low.at[:, block_rows(scal, k, rows)], pieces[2 * k + h].at[4 * rows :, 0:rows])
            for k in range(count)
            for h in range(2)
        ]
        wait_all(copies + start_all(pairs, sems, 10 * count))

    return run_kernel(
        body,
        "mix_weights",
        [(scal, "s"), (normed, "v"), (triple, "v"), (mixed, "v"), (branch_grad, "v")]
        + [(v, "v") for v in sums],
        group_shapes((4 * rows + extra, GROUP), count),
        [
            pltpu.VMEM((width, inner), BF16),
            pltpu.VMEM((2 * GROUP, width), BF16),
            pltpu.VMEM((extra, width), F32),
            pltpu.VMEM((extra, width), BF16),
            pltpu.VMEM((8, inner), F32),
            pltpu.SemaphoreType.DMA((12 * count,)),
        ],
        2 * tokens * width * (inner + 2 * GROUP),
        deps=deps,
    )


def add_kernel(left, right, deps):
    def body(left, right, made):
        made[...] = add_low(left[...], right[...])

    return run_kernel(
        body,
        "add_kernel",
        [(left, "v"), (right, "v")],
        [(left.shape, BF16, "v")],
        [],
        left.size,
        deps=deps,
    )[0]


def input_backward(hidden, own, other, residual_grad, vectors):
    tokens, width = hidden.shape

    def body(hidden, own, other, residual_grad, vectors, input_grad, low_grad, sums):
        sums[...] = jnp.zeros_like(sums)

        @pl.loop(0, tokens // ROWS)
        def _(i):
            part = pl.ds(pl.multiple_of(i * ROWS, ROWS), ROWS)
            grad = own[part, :] + other[part, :].astype(F32)
            back, unit = norm_back(hidden[part, :].astype(F32), vectors[0:1, :], grad)
            sums[0:1, :] += column_sum(grad * unit)
            sums[1:2, :] += column_sum(grad)
            back = residual_grad[part, :] + back
            input_grad[part, :] = back
            low_grad[part, :] = back.astype(BF16)

    return run_kernel(
        body,
        "input_backward",
        [(hidden, "v"), (own, "v"), (other, "v"), (residual_grad, "v"), (vectors, "v")],
        [((tokens, width), F32, "v"), ((tokens, width), BF16, "v"), ((8, width), F32, "v")],
        [],
        20 * tokens * width,
    )


def swap(value, axis, bit):
    count = lax.axis_size(axis)
    return lax.ppermute(value, axis, [(i, i ^ bit) for i in range(count)])


def add_low(left, right):
    return (left.astype(F32) + right.astype(F32)).astype(BF16)


def gather_blocks(halves, bits):
    places = [1 << i for i in range(len(bits))]
    held, stages = {}, ([], [], [])
    for h, value in enumerate(halves):
        order = list(zip(bits, places))
        order = order if h == 0 else order[::-1]
        blocks = {0: value}
        for hop, (bit, place) in enumerate(order):
            for k in list(blocks):
                blocks[k ^ place] = swap(blocks[k], "fsdp", bit)
                stages[0 if hop == 0 else 1 if k == 0 else 2].append(blocks[k ^ place])
        for k in blocks:
            held[k, h] = blocks[k]
    return [held[k, h] for k in range(1 << len(bits)) for h in range(2)], stages


def scatter_blocks(groups, bits, deps=()):
    results, stages, groups = [], [[] for _ in bits], list(groups)
    for h in range(2):
        held = [groups.pop(0) for _ in range(len(bits) + 1)]
        for hop, bit in enumerate(bits if h == 0 else bits[::-1]):
            far = swap(held.pop(0), "fsdp", bit)
            stages[hop].append(far)
            at = 0
            for i, value in enumerate(held):
                if deps and hop == len(bits) - 1:
                    held[i] = add_kernel(value, far, deps)
                else:
                    held[i] = add_low(value, far[at : at + value.shape[0]])
                at += value.shape[0]
        results.append(held[0])
    return results, stages


def sum_line(value):
    place = lax.axis_index("seq")
    inward = lax.ppermute(value, "seq", [(0, 1), (3, 2)])
    near = add_low(value, inward)
    across = lax.ppermute(near, "seq", [(1, 2), (2, 1)])
    both = add_low(near, across)
    back = lax.ppermute(both, "seq", [(1, 0), (2, 3)])
    return jnp.where((place == 1) | (place == 2), both, back), (inward, across, back)


def sum_shares(shares, layer):
    if layer == 0:
        lines = [sum_line(v) for v in shares]
        return [v for v, _ in lines], [moved for _, moved in lines]
    total, moved = sum_line(jnp.concatenate(shares, axis=0))
    size = shares[0].shape[0]
    return [total[:size], total[size:]], [moved]


def pick(flag, first, second):
    return jnp.where(flag, first, second)


def side_pick(core, low, high):
    return jnp.where(core == 0, low, high), jnp.where(core == 0, high, low)


def pack_mix(params, mix, out, vectors, scal):
    rows, count = params
    width = out.shape[1]
    lanes = width // (2 * count)
    half = rows // 2
    extra = vectors.shape[0]

    def body(scal, mix, out, vectors, *made):
        core = scal[3]
        for h in range(2):
            kept, sent = made[h], made[2 + h]
            for t in range(3):
                sides = []
                for s in range(2):
                    blocks = range(h * count // 2, (h + 1) * count // 2)
                    at = [t * width + (2 * b + s) * lanes for b in blocks]
                    sides.append(jnp.concatenate([mix[:, i : i + lanes] for i in at], axis=1))
                part = slice(t * rows, (t + 1) * rows)
                kept[part, :], sent[part, :] = side_pick(core, *sides)
            for j in range(2):
                columns = slice((2 * h + j) * GROUP, (2 * h + j + 1) * GROUP)
                part = slice(3 * rows + j * half, 3 * rows + (j + 1) * half)
                kept[part, :], sent[part, :] = side_pick(
                    core, out[:half, columns], out[half:, columns]
                )
            for target in (kept, sent):
                target[4 * rows :, :] = vectors[...]

    return run_kernel(
        body,
        "pack_mix",
        [(scal, "s"), (mix, "v"), (out, "v"), (vectors, "v")],
        [((4 * rows + extra, GROUP), BF16, "v")] * 4,
        [],
        8 * rows * width,
    )


def pack_feed(params, up, down, scal, deps):
    rows, count = params
    inner, width = up.shape[1], down.shape[1]
    lanes = inner // (2 * count)
    wide, narrow = inner // 8, width // 2

    def body(scal, up, down, *made):
        core = scal[3]
        for h in range(2):
            kept, sent = made[h], made[2 + h]
            for j in range(2):
                sides = []
                for s in range(2):
                    first = (2 * h + j) * wide // lanes
                    at = [(2 * (first + q) + s) * lanes for q in range(wide // lanes)]
                    sides.append(jnp.concatenate([up[:, i : i + lanes] for i in at], axis=1))
                part = slice(j * rows, (j + 1) * rows)
                kept[part, :], sent[part, :] = side_pick(core, *sides)
            columns = slice(h * narrow, (h + 1) * narrow)
            part = slice(2 * rows, 4 * rows)
            kept[part, :], sent[part, :] = side_pick(
                core, down[: 2 * rows, columns], down[2 * rows :, columns]
            )

    return run_kernel(
        body,
        "pack_feed",
        [(scal, "s"), (up, "v"), (down, "v")],
        [((4 * rows, wide), BF16, "v")] * 4,
        [],
        8 * rows * inner,
        deps=deps,
    )


def take_vectors(params, pieces, scal):
    rows, count = params
    width = rows * count
    first = 4 * rows
    extra = pieces[0].shape[0] - first

    def body(scal, *rest):
        pieces, (made, up_bias, mix_bias, held, sems) = rest[:count], rest[count:]
        pairs = [
            (pieces[k].at[first : first + extra, 0:rows], held.at[:, block_rows(scal, k, rows)])
            for k in range(count)
        ]
        wait_all(start_all(pairs, sems))
        made[...] = held[...].astype(F32)
        low = scal[3] == 0
        half = rows // 2
        for b in range(count):
            at = b * rows
            for j in range(2):
                columns = slice((2 * b + j) * rows, (2 * b + j + 1) * rows)
                up_bias[:, columns] = jnp.where(
                    low, made[10 + j : 11 + j, at : at + rows], made[12 + j : 13 + j, at : at + rows]
                )
        for index, t in ((2, 0), (3, 2)):
            row = made[index : index + 1, :]
            parts = [
                jnp.where(
                    low,
                    row[:, b * rows : b * rows + half],
                    row[:, b * rows + half : (b + 1) * rows],
                )
                for b in range(count)
            ]
            joint = jnp.concatenate(parts, axis=1)
            for h in range(2):
                at = (3 * h + t) * GROUP
                mix_bias[:, at : at + GROUP] = joint[:, h * GROUP : (h + 1) * GROUP]
        for h in range(2):
            at = (3 * h + 1) * GROUP
            mix_bias[:, at : at + GROUP] = jnp.zeros((1, GROUP), F32)

    return run_kernel(
        body,
        "take_vectors",
        [(scal, "s")] + [(pieces[2 * k], "a") for k in range(count)],
        [((extra, width), F32, "v"), ((1, 2 * width), F32, "v"), ((1, 6 * GROUP), F32, "v")],
        [pltpu.VMEM((extra, width), BF16), pltpu.SemaphoreType.DMA((count,))],
        width,
    )


def unpack_mix(params, own, far, scal, dtype):
    rows, count = params
    width = rows * count
    lanes = width // (2 * count)
    half = rows // 2
    extra = own[0].shape[0] - 4 * rows

    def body(scal, own0, own1, far0, far1, mix, out, vectors):
        for h, (mine, other) in enumerate(((own0, far0), (own1, far1))):
            for t in range(3):
                part = slice(t * rows, (t + 1) * rows)
                for s, value in enumerate(side_pick(scal[3], mine[part, :], other[part, :])):
                    value = value.astype(dtype)
                    for q in range(count // 2):
                        at = t * width + (2 * (h * count // 2 + q) + s) * lanes
                        mix[:, at : at + lanes] = value[:, q * lanes : (q + 1) * lanes]
            for j in range(2):
                part = slice(3 * rows + j * half, 3 * rows + (j + 1) * half)
                columns = slice((2 * h + j) * GROUP, (2 * h + j + 1) * GROUP)
                for s, value in enumerate(side_pick(scal[3], mine[part, :], other[part, :])):
                    out[s * half : (s + 1) * half, columns] = value.astype(dtype)
        sides = side_pick(scal[3], own0[4 * rows :, :], far0[4 * rows :, :])
        for s, value in enumerate(sides):
            vectors[s * extra : (s + 1) * extra, :] = value.astype(F32)

    return run_kernel(
        body,
        "unpack_mix",
        [(scal, "s")] + [(v, "v") for v in own + far],
        [
            ((rows, 3 * width), dtype, "v"),
            ((rows, width), dtype, "v"),
            ((2 * extra, GROUP), F32, "v"),
        ],
        [],
        8 * rows * width,
    )


def unpack_feed(params, own, far, scal, dtype):
    rows, count = params
    width = rows * count
    wide = own[0].shape[1]
    inner = 8 * wide
    lanes = inner // (2 * count)

    def body(scal, own0, own1, far0, far1, up, down):
        for h, (mine, other) in enumerate(((own0, far0), (own1, far1))):
            for j in range(2):
                part = slice(j * rows, (j + 1) * rows)
                for s, value in enumerate(side_pick(scal[3], mine[part, :], other[part, :])):
                    value = value.astype(dtype)
                    for q in range(wide // lanes):
                        at = (2 * ((2 * h + j) * wide // lanes + q) + s) * lanes
                        up[:, at : at + lanes] = value[:, q * lanes : (q + 1) * lanes]
            part = slice(2 * rows, 4 * rows)
            for s, value in enumerate(side_pick(scal[3], mine[part, :], other[part, :])):
                at = s * 2 * rows
                down[at : at + 2 * rows, h * wide : (h + 1) * wide] = value.astype(dtype)

    return run_kernel(
        body,
        "unpack_feed",
        [(scal, "s")] + [(v, "v") for v in own + far],
        [((rows, inner), dtype, "v"), ((4 * rows, width), dtype, "v")],
        [],
        8 * rows * inner,
    )


def body(activations, cotangent, lengths, *weights):
    mixgain, mixshift, mixweight, mixbias, outweight, outbias, mixscale = weights[:7]
    feedgain, feedshift, upweight, upbias, downweight, downbias, feedscale = weights[7:]
    core, line, spot = (lax.axis_index(a) for a in ("section", "seq", "fsdp"))
    first = core == 0
    parity, micro = line % 2, line // 2
    shards = lax.axis_size("fsdp")
    width = activations.shape[-1]
    inner = upbias.shape[1] * shards
    base_rows = width // shards

    joined, rows = 0, base_rows
    while rows // 2 < HEAD_DIM:
        joined, rows = joined + 1, rows * 2
    count = shards >> joined
    bits = [1 << (joined + i) for i in range(count.bit_length() - 1)]
    params = (rows, count)
    block = spot >> joined

    def join(value, axis=0):
        for i in range(joined):
            far = swap(value, "fsdp", 1 << i)
            upper = ((spot >> i) & 1) == 1
            value = jnp.concatenate([pick(upper, far, value), pick(upper, value, far)], axis=axis)
        return value

    def unjoin(value):
        for i in reversed(range(joined)):
            half = value.shape[0] // 2
            upper = ((spot >> i) & 1) == 1
            low, high = value[:half], value[half:]
            value = add_low(pick(upper, high, low), swap(pick(upper, low, high), "fsdp", 1 << i))
        return value.astype(F32)[None]

    low_micro = micro == 0
    length = pick(low_micro, lengths[0, 0], lengths[1, 0])
    scal = jnp.stack([block, parity, length, core]).astype(jnp.int32)

    def spread(packs):
        layers = [[], []]
        for h in range(2):
            keep, far = packs[h], swap(packs[2 + h], "section", 1)
            layers[0].append(pick(first, keep, far))
            layers[1].append(pick(first, far, keep))
        return layers

    vectors = jnp.stack(
        [mixgain[0], mixshift[0], mixbias[0, 0], mixbias[0, 1], outbias[0], mixscale[0]]
        + [feedgain[0], feedshift[0], downbias[0], feedscale[0]]
    )
    vectors = jnp.concatenate(
        [join(vectors, 1), join(upbias[0]).reshape(4, rows), jnp.zeros((2, rows), BF16)], axis=0
    )
    if rows < GROUP:
        vectors = jnp.concatenate([vectors, jnp.zeros((16, GROUP - rows), BF16)], axis=1)
    mix_halves = spread(pack_mix(params, join(mixweight[0]), join(outweight[0]), vectors, scal))
    mix_parts = [gather_blocks(halves, bits) for halves in mix_halves]
    mix_pieces, mix_stages = zip(*mix_parts)
    ready = mix_stages[0][0] + mix_stages[0][1]
    feed_halves = spread(
        pack_feed(params, join(upweight[0]), join(downweight[0]), scal, ready)
    )
    feed_parts = [gather_blocks(halves, bits) for halves in feed_halves]
    feed_pieces, feed_stages = zip(*feed_parts)

    tokens = activations.shape[2]

    def to_pair(value):
        keep = pick(low_micro, value[0, 0], value[1, 0])
        far = swap(pick(low_micro, value[1, 0], value[0, 0]), "seq", 2)
        return jnp.concatenate([pick(low_micro, keep, far), pick(low_micro, far, keep)], axis=0)

    def from_pair(value):
        low, high = value[:tokens], value[tokens:]
        far = swap(pick(low_micro, high, low).astype(BF16), "seq", 2)
        wide = far.astype(value.dtype)
        keep = pick(low_micro, low, high)
        made = jnp.stack([pick(low_micro, keep, wide), pick(low_micro, wide, keep)])
        return made[None, :, None], far

    hidden = to_pair(activations)
    incoming = to_pair(cotangent)
    kept, results = [], []
    for layer in range(2):
        pieces, feeds = mix_pieces[layer], feed_pieces[layer]
        vectors, up_bias, mix_bias = take_vectors(params, pieces, scal)
        normed, keep, send = mix_forward(params, hidden, vectors, mix_bias, scal, pieces, [])
        other = swap(send, "seq", 1)
        out_keep, out_send, peaks = attend_forward(
            keep, other, scal, feed_stages[layer][0] + feed_stages[layer][1] + [incoming]
        )
        out_other = swap(out_send, "seq", 1)
        mixed, own, send = out_forward(
            params, out_keep, out_other, scal, pieces, width, feed_stages[layer][2]
        )
        far = swap(send, "section", 1)
        branch, residual, normed_two, active, slope, own, send = feed_forward(
            params, hidden, own, far, vectors, up_bias, scal, feeds,
            mix_stages[1][0] + mix_stages[1][1] if layer == 0 else [],
        )
        far = swap(send, "section", 1)
        kept.append(
            (hidden, normed, keep, other, peaks, mixed, branch, residual, normed_two, active)
            + (slope, own, far, vectors)
        )
        hidden = layer_result(
            residual, own, far, vectors,
            mix_stages[1][2] + feed_stages[1][0] if layer == 0 else [],
        )
        results.append(hidden)

    section_output, sent = from_pair(pick(first, results[0], results[1]))
    gradients, mix_shares, feed_shares = [None] * 2, [None] * 2, [None] * 2
    waits = {"attend": [sent]}
    for layer in (1, 0):
        pieces, feeds = mix_pieces[layer], feed_pieces[layer]
        hidden, normed, keep, other, peaks, mixed, branch, residual, normed_two, active = kept[
            layer
        ][:10]
        slope, branch_own, branch_far, vectors = kept[layer][10:]
        lower, up_grad, up_sum, own, send = feed_backward(
            params, incoming, vectors, slope, scal, feeds, waits.get("feed", [])
        )
        far = swap(send, "section", 1)
        grads = feed_weights(params, active, lower, normed_two, up_grad, scal, [branch_far])
        feed_share, feed_hops = scatter_blocks(grads, bits)
        feed_shares[layer], feed_lines = sum_shares(feed_share, layer)
        feed_sum = feed_sums(incoming, branch_own, branch_far, vectors, lower)
        residual_grad, branch_grad, grad_keep, grad_send, out_sum = out_backward(
            params, incoming, residual, own, far, branch, vectors, scal, pieces, waits.get("out", [])
        )
        grad_other = swap(grad_send, "seq", 1)
        triple_keep, triple_send = attend_backward(
            keep, other, grad_keep, grad_other, peaks, scal, waits.get("attend", [])
        )
        triple_other = swap(triple_send, "seq", 1)
        triple, own, send = mix_backward(
            params, triple_keep, triple_other, scal, pieces, width, waits.get("mix", []) + feed_hops[0]
        )
        far = swap(send, "section", 1)
        input_grad, incoming, in_sum = input_backward(hidden, own, far, residual_grad, vectors)
        gradients[layer] = input_grad
        after = []
        if layer == 0:
            input_gradient, sent = from_pair(pick(first, gradients[0], gradients[1]))
            after = [sent]
        grads = mix_weights(
            params, normed, triple, mixed, branch_grad, [in_sum, out_sum, feed_sum, up_sum], scal,
            waits.get("weights", []) + (feed_hops[1] if layer == 0 else []),
        )
        mix_share, mix_hops = scatter_blocks(grads, bits, after)
        mix_shares[layer], mix_lines = sum_shares(mix_share, layer)
        waits = {
            "feed": sum(feed_hops[1:], []),
            "out": mix_hops[0],
            "attend": sum(mix_hops[1:], []),
            "mix": [moved[0] for moved in feed_lines],
            "weights": [moved[1] for moved in feed_lines] + [moved[0] for moved in mix_lines],
        }

    def collect(unpack, shares):
        own = [pick(first, low, high) for low, high in zip(*shares)]
        far = [swap(pick(first, high, low), "section", 1) for low, high in zip(*shares)]
        return unpack(params, own, far, scal, BF16 if joined else F32)

    up_weight, down_weight = (unjoin(v) for v in collect(unpack_feed, feed_shares))
    *made, sums = collect(unpack_mix, mix_shares)
    mix_total, out_total = (unjoin(v) for v in made)

    extra = sums.shape[0] // 2
    sums = sums[:, :rows].reshape(2, extra, rows)
    place = spot & ((1 << joined) - 1)

    def own_part(value):
        size = value.shape[-1] >> joined
        return lax.dynamic_slice_in_dim(value, place * size, size, axis=value.ndim - 1)

    whole = own_part(sums[0, :8])[:, None]
    up_total = own_part(sums[:, 8:10].reshape(1, 4 * rows))
    bias_total = sums[:, 10].reshape(2, 2, rows // 2).transpose(1, 0, 2).reshape(2, rows)
    bias_total = own_part(bias_total)[None]

    return (
        section_output,
        input_gradient,
        whole[0],
        whole[1],
        mix_total,
        bias_total,
        out_total,
        whole[5],
        whole[4],
        whole[2],
        whole[3],
        up_weight,
        up_total,
        down_weight,
        whole[7],
        whole[6],
    )


def solution(mesh):
    rowed, flat = P("section", "fsdp", None), P("section", "fsdp")
    image = P(None, "fsdp", "seq", None)
    bias = P("section", None, "fsdp")
    kept = P("section", None, "fsdp", "seq", None)
    params = (flat, flat, rowed, bias, rowed, flat, flat, flat, flat, rowed, flat, rowed, flat, flat)
    return jax.shard_map(
        body,
        mesh=mesh,
        in_specs=(image, image, P(None, "fsdp")) + params,
        out_specs=(kept, kept) + params,
        check_vma=False,
    )
```

```python
import math

import jax
import jax.numpy as jnp
from jax import lax
from jax.experimental import pallas as pl
from jax.experimental.pallas import tpu as pltpu
from jax.sharding import PartitionSpec as P

HEAD_DIM = 64
EPSILON = 1e-06
NEGATIVE = -1000000000.0
F32 = jnp.float32
BF16 = jnp.bfloat16
GROUP = 256
MIN_LENGTH = 896
CHUNK = 256
ROWS = 64
MIB = 1024 * 1024


def dot_nn(left, right):
    return lax.dot_general(left, right, (((1,), (0,)), ((), ())), preferred_element_type=F32)


def dot_nt(left, right):
    return lax.dot_general(left, right, (((1,), (1,)), ((), ())), preferred_element_type=F32)


def dot_tn(left, right):
    return lax.dot_general(left, right, (((0,), (0,)), ((), ())), preferred_element_type=F32)


def size_of(shape, dtype):
    return math.prod(shape) * jnp.dtype(dtype).itemsize


def run_kernel(kernel, name, ins, outs, scratch, flops, exps=0, deps=()):
    deps = list(deps)

    def body(*refs):
        kernel(*refs[len(deps) :])

    spaces = {"v": pltpu.VMEM, "a": pl.ANY, "s": pltpu.SMEM}
    moved = sum(size_of(a.shape, a.dtype) for a, _ in ins) + sum(size_of(s, d) for s, d, _ in outs)
    held = sum(size_of(a.shape, a.dtype) for a, k in ins if k == "v")
    ins = [(a, "a") for a in deps] + ins
    held += sum(size_of(s, d) for s, d, k in outs if k == "v")
    held += sum(size_of(s.shape, s.dtype) for s in scratch if s.memory_space == pltpu.VMEM)
    return pl.pallas_call(
        body,
        name=name,
        out_shape=[jax.ShapeDtypeStruct(s, d) for s, d, _ in outs],
        in_specs=[pl.BlockSpec(memory_space=spaces[k]) for _, k in ins],
        out_specs=[pl.BlockSpec(memory_space=spaces[k]) for _, _, k in outs],
        scratch_shapes=scratch,
        compiler_params=pltpu.CompilerParams(vmem_limit_bytes=min(held + 14 * MIB, 58 * MIB)),
        cost_estimate=pl.CostEstimate(flops=flops // 16, bytes_accessed=moved // 16, transcendentals=0),
    )(*[a for a, _ in ins])


def start_all(pairs, sems, first=0):
    copies = []
    for index, (source, target) in enumerate(pairs):
        copies.append(pltpu.make_async_copy(source, target, sems.at[first + index]))
        copies[-1].start()
    return copies


def wait_all(copies):
    for copy in copies:
        copy.wait()


def block_rows(scal, k, rows):
    return pl.ds(pl.multiple_of((scal[0] ^ k) * rows, rows), rows)


def scatter_groups(count, h):
    places = [1 << i for i in range(count.bit_length() - 1)]
    groups = [[0]]
    for place in places[::-1] if h == 0 else places:
        groups.insert(0, [k ^ place for group in groups for k in group])
    return groups


def group_shapes(shape, count):
    return [
        ((len(group) * shape[0], shape[1]), BF16, "a")
        for h in range(2)
        for group in scatter_groups(count, h)
    ]


def group_views(refs, size, count):
    views, refs = {}, list(refs)
    for h in range(2):
        for group in scatter_groups(count, h):
            ref = refs.pop(0)
            for place, k in enumerate(group):
                views[2 * k + h] = ref.at[place * size : (place + 1) * size, :]
    return [views[i] for i in range(2 * count)]


def mix_pairs(scal, pieces, full, rows, count):
    return [
        (
            pieces[2 * k + h].at[t * rows : (t + 1) * rows, :],
            full.at[block_rows(scal, k, rows), (3 * h + t) * GROUP : (3 * h + t + 1) * GROUP],
        )
        for k in range(count)
        for h in range(2)
        for t in range(3)
    ]


def out_pairs(scal, pieces, full, rows, count):
    half = rows // 2
    return [
        (
            pieces[2 * k + h].at[3 * rows + j * half : 3 * rows + (j + 1) * half, :],
            full.at[block_rows(scal, k, half), (2 * h + j) * GROUP : (2 * h + j + 1) * GROUP],
        )
        for k in range(count)
        for h in range(2)
        for j in range(2)
    ]


def up_pairs(scal, pieces, full, rows, count):
    width = pieces[0].shape[1]
    return [
        (
            pieces[2 * k + h].at[j * rows : (j + 1) * rows, :],
            full.at[block_rows(scal, k, rows), (2 * h + j) * width : (2 * h + j + 1) * width],
        )
        for k in range(count)
        for h in range(2)
        for j in range(2)
    ]


def down_pairs(scal, pieces, full, rows, count):
    width = pieces[0].shape[1]
    return [
        (
            pieces[2 * k + h].at[2 * rows : 4 * rows, :],
            full.at[block_rows(scal, k, 2 * rows), h * width : (h + 1) * width],
        )
        for k in range(count)
        for h in range(2)
    ]


def norm_parts(values):
    center = jnp.mean(values, axis=-1, keepdims=True)
    centered = values - center
    spread = jnp.mean(centered * centered, axis=-1, keepdims=True)
    inverse = lax.rsqrt(spread + EPSILON)
    return centered * inverse, inverse


def norm_back(values, gain, grad):
    unit, inverse = norm_parts(values)
    scaled = grad * gain
    mean_one = jnp.mean(scaled, axis=-1, keepdims=True)
    mean_two = jnp.mean(scaled * unit, axis=-1, keepdims=True)
    return inverse * (scaled - mean_one - unit * mean_two), unit


def column_sum(values):
    return jnp.sum(values, axis=0, keepdims=True)


def gelu_pair(values):
    energy = jnp.exp(values * values * -0.5)
    t = 1.0 / (1.0 + (0.3275911 * 0.7071067811865476) * jnp.abs(values))
    tail = 1.061405429 * 0.5
    for factor in (-1.453152027, 1.421413741, -0.284496736, 0.254829592):
        tail = tail * t + factor * 0.5
    tail = tail * t * energy
    below = jnp.where(values >= 0, 1.0 - tail, tail)
    return values * below, below + values * energy * 0.3989422804014327


def mix_forward(params, hidden, vectors, bias, scal, pieces, deps):
    rows, count = params
    tokens, width = hidden.shape
    span = 3 * GROUP

    def body(scal, hidden, vectors, bias, *rest):
        pieces, (normed, keep, send, full, sems) = rest[: 2 * count], rest[2 * count :]
        copies = start_all(mix_pairs(scal, pieces, full, rows, count), sems)

        @pl.loop(0, tokens // ROWS)
        def _(i):
            part = pl.ds(pl.multiple_of(i * ROWS, ROWS), ROWS)
            unit, _ = norm_parts(hidden[part, :].astype(F32))
            normed[part, :] = (unit * vectors[0:1, :] + vectors[1:2, :]).astype(BF16)

        wait_all(copies)
        for target, group in ((send, 1 - scal[1]), (keep, scal[1])):
            for t in range(3):
                columns = pl.ds(pl.multiple_of((group * 3 + t) * GROUP, GROUP), GROUP)
                made = dot_nn(normed[...], full[:, columns]) + bias[:, columns]
                target[:, t * GROUP : (t + 1) * GROUP] = made.astype(BF16)

    return run_kernel(
        body,
        "mix_forward",
        [(scal, "s"), (hidden, "v"), (vectors, "v"), (bias, "v")] + [(p, "a") for p in pieces],
        [((tokens, width), BF16, "v"), ((tokens, span), BF16, "v"), ((tokens, span), BF16, "v")],
        [pltpu.VMEM((width, 2 * span), BF16), pltpu.SemaphoreType.DMA((6 * count,))],
        4 * tokens * width * span,
        deps=deps,
    )


def place_tokens(scal, keep, other, full, sems, first=0):
    tokens = keep.shape[0]
    own = pl.ds(pl.multiple_of(scal[1] * tokens, tokens), tokens)
    far = pl.ds(pl.multiple_of((1 - scal[1]) * tokens, tokens), tokens)
    return start_all([(keep, full.at[own, :]), (other, full.at[far, :])], sems, first)


def split_tokens(scal, full, keep, send, sems):
    tokens = keep.shape[0]
    own = pl.ds(pl.multiple_of(scal[1] * tokens, tokens), tokens)
    far = pl.ds(pl.multiple_of((1 - scal[1]) * tokens, tokens), tokens)
    wait_all(start_all([(full.at[far, :], send), (full.at[own, :], keep)], sems))


def masked(scores, length):
    start = MIN_LENGTH
    tail = scores[start:, :]
    position = lax.broadcasted_iota(jnp.int32, tail.shape, 0) + start
    return scores[:start, :], jnp.where(position < length, tail, NEGATIVE)


def attend_forward(keep, other, scal, deps):
    tokens = keep.shape[0]
    total = 2 * tokens
    heads = GROUP // HEAD_DIM

    def body(scal, keep, other, out_keep, out_send, peaks, full, out, sems):
        wait_all(place_tokens(scal, keep, other, full, sems))
        length = scal[2]
        for pair in range(heads // 2):

            @pl.loop(0, total // CHUNK)
            def _(i):
                part = pl.ds(pl.multiple_of(i * CHUNK, CHUNK), CHUNK)
                outs = []
                for head in (2 * pair, 2 * pair + 1):
                    at = head * HEAD_DIM
                    query = full[part, at : at + HEAD_DIM] * jnp.asarray(HEAD_DIM**-0.5, BF16)
                    key = full[:, GROUP + at : GROUP + at + HEAD_DIM]
                    value = full[:, 2 * GROUP + at : 2 * GROUP + at + HEAD_DIM]
                    low, high = masked(dot_nt(key, query), length)
                    peak = jnp.maximum(
                        jnp.max(low, axis=0, keepdims=True), jnp.max(high, axis=0, keepdims=True)
                    )
                    low = jnp.exp(low - peak)
                    high = jnp.exp(high - peak)
                    mass = column_sum(low) + column_sum(high)
                    probs = jnp.concatenate([low.astype(BF16), high.astype(BF16)], axis=0)
                    outs.append(dot_tn(value, probs) / mass)
                    peaks[head : head + 1, part] = peak + jnp.log(mass)
                made = jnp.concatenate(outs, axis=0)
                out[part, pair * 128 : (pair + 1) * 128] = made.T.astype(BF16)

        split_tokens(scal, out, out_keep, out_send, sems)

    return run_kernel(
        body,
        "attend_forward",
        [(scal, "s"), (keep, "a"), (other, "a")],
        [
            ((tokens, GROUP), BF16, "a"),
            ((tokens, GROUP), BF16, "a"),
            ((8, total), F32, "v"),
        ],
        [
            pltpu.VMEM((total, 3 * GROUP), BF16),
            pltpu.VMEM((total, GROUP), BF16),
            pltpu.SemaphoreType.DMA((2,)),
        ],
        heads * total * total * HEAD_DIM * 4,
        heads * total * total,
        deps,
    )


def place_groups(scal, keep, other, full, sems, first=0):
    width = keep.shape[1]
    own = pl.ds(pl.multiple_of(scal[1] * width, width), width)
    far = pl.ds(pl.multiple_of((1 - scal[1]) * width, width), width)
    return start_all([(keep, full.at[:, own]), (other, full.at[:, far])], sems, first)


def out_forward(params, keep, other, scal, pieces, width, deps):
    rows, count = params
    tokens = keep.shape[0]
    inner = 2 * GROUP

    def body(scal, keep, other, *rest):
        pieces, (mixed, own, send, full, sems) = rest[: 2 * count], rest[2 * count :]
        copies = place_groups(scal, keep, other, mixed, sems)
        copies += start_all(out_pairs(scal, pieces, full, rows, count), sems, 2)
        wait_all(copies)
        for j in range(width // GROUP):
            columns = slice(j * GROUP, (j + 1) * GROUP)
            made = dot_nn(mixed[...], full[:, columns])
            own[:, columns] = made
            send[:, columns] = made.astype(BF16)

    return run_kernel(
        body,
        "out_forward",
        [(scal, "s"), (keep, "a"), (other, "a")] + [(p, "a") for p in pieces],
        [((tokens, inner), BF16, "v"), ((tokens, width), F32, "v"), ((tokens, width), BF16, "v")],
        [pltpu.VMEM((inner, width), BF16), pltpu.SemaphoreType.DMA((4 * count + 2,))],
        2 * tokens * inner * width,
        deps=deps,
    )


def feed_forward(params, hidden, own, other, vectors, upbias, scal, pieces, deps):
    rows, count = params
    tokens, width = hidden.shape
    inner = upbias.shape[1]
    tile = 512

    def body(scal, hidden, own, other, vectors, upbias, *rest):
        pieces = rest[: 2 * count]
        branch, residual, normed, active, slope, made_own, made_send, up, down, sems = rest[
            2 * count :
        ]
        up_copies = start_all(up_pairs(scal, pieces, up, rows, count), sems)
        down_copies = start_all(down_pairs(scal, pieces, down, rows, count), sems, 4 * count)

        @pl.loop(0, tokens // ROWS)
        def _(i):
            part = pl.ds(pl.multiple_of(i * ROWS, ROWS), ROWS)
            made = own[part, :] + other[part, :].astype(F32) + vectors[4:5, :]
            branch[part, :] = made
            made = hidden[part, :].astype(F32) + vectors[5:6, :] * made
            residual[part, :] = made
            unit, _ = norm_parts(made)
            normed[part, :] = (unit * vectors[6:7, :] + vectors[7:8, :]).astype(BF16)

        wait_all(up_copies)

        @pl.loop(0, inner // tile)
        def _(i):
            columns = pl.ds(pl.multiple_of(i * tile, tile), tile)
            for r in range(tokens // 256):
                part = slice(r * 256, (r + 1) * 256)
                made = dot_nn(normed[part, :], up[:, columns]) + upbias[:, columns]
                value, gradient = gelu_pair(made)
                active[part, columns] = value.astype(BF16)
                slope[part, columns] = gradient.astype(BF16)

        wait_all(down_copies)

        @pl.loop(0, width // GROUP)
        def _(i):
            columns = pl.ds(pl.multiple_of(i * GROUP, GROUP), GROUP)
            made = dot_nn(active[...], down[:, columns])
            made_own[:, columns] = made
            made_send[:, columns] = made.astype(BF16)

    return run_kernel(
        body,
        "feed_forward",
        [(scal, "s"), (hidden, "v"), (own, "v"), (other, "v"), (vectors, "v"), (upbias, "v")]
        + [(p, "a") for p in pieces],
        [
            ((tokens, width), F32, "v"),
            ((tokens, width), F32, "v"),
            ((tokens, width), BF16, "v"),
            ((tokens, inner), BF16, "v"),
            ((tokens, inner), BF16, "v"),
            ((tokens, width), F32, "v"),
            ((tokens, width), BF16, "v"),
        ],
        [
            pltpu.VMEM((width, inner), BF16),
            pltpu.VMEM((inner, width), BF16),
            pltpu.SemaphoreType.DMA((6 * count,)),
        ],
        4 * tokens * width * inner,
        2 * tokens * inner,
        deps,
    )


def layer_result(residual, own, other, vectors, deps):
    tokens, width = residual.shape

    def body(residual, own, other, vectors, made):
        @pl.loop(0, tokens // ROWS)
        def _(i):
            part = pl.ds(pl.multiple_of(i * ROWS, ROWS), ROWS)
            branch = own[part, :] + other[part, :].astype(F32) + vectors[8:9, :]
            made[part, :] = (residual[part, :] + vectors[9:10, :] * branch).astype(BF16)

    return run_kernel(
        body,
        "layer_result",
        [(residual, "v"), (own, "v"), (other, "v"), (vectors, "v")],
        [((tokens, width), BF16, "v")],
        [],
        4 * tokens * width,
        deps=deps,
    )[0]


def feed_backward(params, incoming, vectors, slope, scal, pieces, deps):
    rows, count = params
    tokens, width = incoming.shape
    inner = slope.shape[1]
    tile = 512

    def body(scal, incoming, vectors, slope, *rest):
        pieces = rest[: 2 * count]
        lower, up_grad, bias_grad, made_own, made_send, up, down, sems = rest[2 * count :]
        down_copies = start_all(down_pairs(scal, pieces, down, rows, count), sems)
        up_copies = start_all(up_pairs(scal, pieces, up, rows, count), sems, 2 * count)

        @pl.loop(0, tokens // ROWS)
        def _(i):
            part = pl.ds(pl.multiple_of(i * ROWS, ROWS), ROWS)
            lower[part, :] = (incoming[part, :].astype(F32) * vectors[9:10, :]).astype(BF16)

        wait_all(down_copies)

        @pl.loop(0, inner // tile)
        def _(i):
            columns = pl.ds(pl.multiple_of(i * tile, tile), tile)
            made = dot_nt(lower[...], down[columns, :])
            made = (made * slope[:, columns].astype(F32)).astype(BF16)
            up_grad[:, columns] = made
            bias_grad[:, columns] = column_sum(made.astype(F32))

        wait_all(up_copies)

        @pl.loop(0, width // GROUP)
        def _(i):
            columns = pl.ds(pl.multiple_of(i * GROUP, GROUP), GROUP)
            made = dot_nt(up_grad[...], up[columns, :])
            made_own[:, columns] = made
            made_send[:, columns] = made.astype(BF16)

    return run_kernel(
        body,
        "feed_backward",
        [(scal, "s"), (incoming, "v"), (vectors, "v"), (slope, "v")]
        + [(p, "a") for p in pieces],
        [
            ((tokens, width), BF16, "v"),
            ((tokens, inner), BF16, "v"),
            ((1, inner), F32, "v"),
            ((tokens, width), F32, "v"),
            ((tokens, width), BF16, "v"),
        ],
        [
            pltpu.VMEM((width, inner), BF16),
            pltpu.VMEM((inner, width), BF16),
            pltpu.SemaphoreType.DMA((6 * count,)),
        ],
        4 * tokens * width * inner,
        deps=deps,
    )


def feed_weights(params, active, lower, normed, up_grad, scal, deps):
    rows, count = params
    tokens, width = lower.shape
    inner = active.shape[1]
    shape = (4 * rows, inner // 4)
    tile = 512

    def body(scal, active, lower, normed, up_grad, *rest):
        pieces, (up, down, sems) = group_views(rest[:-3], 4 * rows, count), rest[-3:]

        @pl.loop(0, inner // tile)
        def _(i):
            part = pl.ds(pl.multiple_of(i * tile, tile), tile)
            down[part, :] = dot_tn(active[:, part], lower[...]).astype(BF16)

        pairs = [(b, a) for a, b in down_pairs(scal, pieces, down, rows, count)]
        copies = start_all(pairs, sems)

        @pl.loop(0, inner // tile)
        def _(i):
            part = pl.ds(pl.multiple_of(i * tile, tile), tile)
            up[:, part] = dot_tn(normed[...], up_grad[:, part]).astype(BF16)

        pairs = [(b, a) for a, b in up_pairs(scal, pieces, up, rows, count)]
        wait_all(copies + start_all(pairs, sems, 2 * count))

    return run_kernel(
        body,
        "feed_weights",
        [(scal, "s"), (active, "v"), (lower, "v"), (normed, "v"), (up_grad, "v")],
        group_shapes(shape, count),
        [
            pltpu.VMEM((width, inner), BF16),
            pltpu.VMEM((inner, width), BF16),
            pltpu.SemaphoreType.DMA((6 * count,)),
        ],
        4 * tokens * width * inner,
        deps=deps,
    )


def feed_sums(incoming, own, other, vectors, lower):
    tokens, width = incoming.shape

    def body(incoming, own, other, vectors, lower, sums):
        sums[...] = jnp.zeros_like(sums)

        @pl.loop(0, tokens // ROWS)
        def _(i):
            part = pl.ds(pl.multiple_of(i * ROWS, ROWS), ROWS)
            branch = own[part, :] + other[part, :].astype(F32) + vectors[8:9, :]
            sums[0:1, :] += column_sum(branch * incoming[part, :].astype(F32))
            sums[1:2, :] += column_sum(lower[part, :].astype(F32))

    return run_kernel(
        body,
        "feed_sums",
        [(incoming, "v"), (own, "v"), (other, "v"), (vectors, "v"), (lower, "v")],
        [((8, width), F32, "v")],
        [],
        4 * tokens * width,
    )[0]


def out_backward(params, incoming, residual, own, other, branch, vectors, scal, pieces, deps):
    rows, count = params
    tokens, width = incoming.shape
    inner = 2 * GROUP

    def body(scal, incoming, residual, own, other, branch, vectors, *rest):
        pieces = rest[: 2 * count]
        residual_grad, branch_grad, keep, send, sums, full, sems = rest[2 * count :]
        copies = start_all(out_pairs(scal, pieces, full, rows, count), sems)
        sums[...] = jnp.zeros_like(sums)

        @pl.loop(0, tokens // ROWS)
        def _(i):
            part = pl.ds(pl.multiple_of(i * ROWS, ROWS), ROWS)
            grad = own[part, :] + other[part, :].astype(F32)
            back, unit = norm_back(residual[part, :], vectors[6:7, :], grad)
            sums[0:1, :] += column_sum(grad * unit)
            sums[1:2, :] += column_sum(grad)
            back = incoming[part, :].astype(F32) + back
            residual_grad[part, :] = back
            sums[2:3, :] += column_sum(back * branch[part, :])
            low = (back * vectors[5:6, :]).astype(BF16)
            branch_grad[part, :] = low
            sums[3:4, :] += column_sum(low.astype(F32))

        wait_all(copies)
        for target, group in ((send, 1 - scal[1]), (keep, scal[1])):
            part = pl.ds(pl.multiple_of(group * GROUP, GROUP), GROUP)
            target[...] = dot_nt(branch_grad[...], full[part, :]).astype(BF16)

    return run_kernel(
        body,
        "out_backward",
        [(scal, "s"), (incoming, "v"), (residual, "v"), (own, "v"), (other, "v"), (branch, "v")]
        + [(vectors, "v")]
        + [(p, "a") for p in pieces],
        [
            ((tokens, width), F32, "v"),
            ((tokens, width), BF16, "v"),
            ((tokens, GROUP), BF16, "v"),
            ((tokens, GROUP), BF16, "v"),
            ((8, width), F32, "v"),
        ],
        [pltpu.VMEM((inner, width), BF16), pltpu.SemaphoreType.DMA((4 * count,))],
        2 * tokens * inner * width,
        deps=deps,
    )


def attend_backward(keep, other, grad_keep, grad_other, peaks, scal, deps):
    tokens = keep.shape[0]
    total = 2 * tokens
    heads = GROUP // HEAD_DIM

    def body(scal, keep, other, grad_keep, grad_other, peaks, out_keep, out_send, *rest):
        full, grads, out, key_sum, value_sum, sems = rest
        copies = place_tokens(scal, keep, other, full, sems)
        copies += place_tokens(scal, grad_keep, grad_other, grads, sems, 2)
        wait_all(copies)
        length = scal[2]
        for pair in range(heads // 2):
            key_sum[...] = jnp.zeros_like(key_sum)
            value_sum[...] = jnp.zeros_like(value_sum)

            @pl.loop(0, total // CHUNK)
            def _(i):
                part = pl.ds(pl.multiple_of(i * CHUNK, CHUNK), CHUNK)
                query_parts = []
                for side, head in enumerate((2 * pair, 2 * pair + 1)):
                    at = head * HEAD_DIM
                    query = full[part, at : at + HEAD_DIM] * jnp.asarray(HEAD_DIM**-0.5, BF16)
                    key = full[:, GROUP + at : GROUP + at + HEAD_DIM]
                    value = full[:, 2 * GROUP + at : 2 * GROUP + at + HEAD_DIM]
                    grad = grads[part, at : at + HEAD_DIM]
                    low, high = masked(dot_nt(key, query), length)
                    peak = peaks[head : head + 1, part]
                    probs = jnp.concatenate([jnp.exp(low - peak), jnp.exp(high - peak)], axis=0)
                    prob_grad = dot_nt(value, grad)
                    mean = column_sum(probs * prob_grad)
                    score_grad = (probs * (prob_grad - mean)).astype(BF16)
                    lanes = slice(side * HEAD_DIM, (side + 1) * HEAD_DIM)
                    value_sum[:, lanes] += dot_nn(probs.astype(BF16), grad)
                    key_sum[:, lanes] += dot_nn(score_grad, query)
                    query_parts.append(dot_tn(key, score_grad) * HEAD_DIM**-0.5)
                made = jnp.concatenate(query_parts, axis=0)
                out[part, pair * 128 : (pair + 1) * 128] = made.T.astype(BF16)

            at = pair * 128
            out[:, GROUP + at : GROUP + at + 128] = key_sum[...].astype(BF16)
            out[:, 2 * GROUP + at : 2 * GROUP + at + 128] = value_sum[...].astype(BF16)

        split_tokens(scal, out, out_keep, out_send, sems)

    return run_kernel(
        body,
        "attend_backward",
        [(scal, "s"), (keep, "a"), (other, "a"), (grad_keep, "a"), (grad_other, "a")]
        + [(peaks, "v")],
        [((tokens, 3 * GROUP), BF16, "a"), ((tokens, 3 * GROUP), BF16, "a")],
        [
            pltpu.VMEM((total, 3 * GROUP), BF16),
            pltpu.VMEM((total, GROUP), BF16),
            pltpu.VMEM((total, 3 * GROUP), BF16),
            pltpu.VMEM((total, 128), F32),
            pltpu.VMEM((total, 128), F32),
            pltpu.SemaphoreType.DMA((4,)),
        ],
        heads * total * total * HEAD_DIM * 10,
        heads * total * total,
        deps,
    )


def mix_backward(params, keep, other, scal, pieces, width, deps):
    rows, count = params
    tokens = keep.shape[0]
    inner = 6 * GROUP

    def body(scal, keep, other, *rest):
        pieces = rest[: 2 * count]
        triple, own, send, full, sems = rest[2 * count :]
        copies = place_groups(scal, keep, other, triple, sems)
        copies += start_all(mix_pairs(scal, pieces, full, rows, count), sems, 2)
        wait_all(copies)

        @pl.loop(0, width // GROUP)
        def _(i):
            columns = pl.ds(pl.multiple_of(i * GROUP, GROUP), GROUP)
            made = dot_nt(triple[...], full[columns, :])
            own[:, columns] = made
            send[:, columns] = made.astype(BF16)

    return run_kernel(
        body,
        "mix_backward",
        [(scal, "s"), (keep, "a"), (other, "a")] + [(p, "a") for p in pieces],
        [((tokens, inner), BF16, "v"), ((tokens, width), F32, "v"), ((tokens, width), BF16, "v")],
        [pltpu.VMEM((width, inner), BF16), pltpu.SemaphoreType.DMA((6 * count + 2,))],
        2 * tokens * inner * width,
        deps=deps,
    )


def mix_weights(params, normed, triple, mixed, branch_grad, sums, scal, deps):
    rows, count = params
    tokens, width = normed.shape
    inner = triple.shape[1]

    extra, half = 16, rows // 2

    def body(scal, normed, triple, mixed, branch_grad, *rest):
        *in_sums, out_sum, feed_sum, up_sum = rest[: len(sums)]
        refs, (full, out, vectors, low, bias, sems) = rest[len(sums) : -6], rest[-6:]
        pieces = group_views(refs, 4 * rows + extra, count)
        out[...] = dot_tn(mixed[...], branch_grad[...]).astype(BF16)
        pairs = [(b, a) for a, b in out_pairs(scal, pieces, out, rows, count)]
        copies = start_all(pairs, sems)

        @pl.loop(0, inner // GROUP)
        def _(i):
            part = pl.ds(pl.multiple_of(i * GROUP, GROUP), GROUP)
            full[:, part] = dot_tn(normed[...], triple[:, part]).astype(BF16)
            bias[0:1, part] = column_sum(triple[:, part].astype(F32))

        pairs = [(b, a) for a, b in mix_pairs(scal, pieces, full, rows, count)]
        copies += start_all(pairs, sems, 4 * count)
        vectors[...] = jnp.zeros_like(vectors)
        for i, in_sum in enumerate(in_sums):
            at = 11 if i == 0 else 0
            vectors[at : at + 2, :] = in_sum[0:2, :]
        vectors[2:6, :] = out_sum[0:4, :]
        vectors[6:8, :] = feed_sum[0:2, :]
        for j in range(2):
            for b in range(count):
                at = (2 * b + j) * rows
                vectors[8 + j : 9 + j, b * rows : (b + 1) * rows] = up_sum[:, at : at + rows]
        for side, t in enumerate((0, 2)):
            row = jnp.concatenate(
                [bias[0:1, (3 * h + t) * GROUP : (3 * h + t + 1) * GROUP] for h in range(2)], axis=1
            )
            for b in range(count):
                at = b * rows + side * half
                vectors[10:11, at : at + half] = row[:, b * half : (b + 1) * half]
        low[...] = vectors[...].astype(BF16)
        pairs = [
            (low.at[:, block_rows(scal, k, rows)], pieces[2 * k + h].at[4 * rows :, 0:rows])
            for k in range(count)
            for h in range(2)
        ]
        wait_all(copies + start_all(pairs, sems, 10 * count))

    return run_kernel(
        body,
        "mix_weights",
        [(scal, "s"), (normed, "v"), (triple, "v"), (mixed, "v"), (branch_grad, "v")]
        + [(v, "v") for v in sums],
        group_shapes((4 * rows + extra, GROUP), count),
        [
            pltpu.VMEM((width, inner), BF16),
            pltpu.VMEM((2 * GROUP, width), BF16),
            pltpu.VMEM((extra, width), F32),
            pltpu.VMEM((extra, width), BF16),
            pltpu.VMEM((8, inner), F32),
            pltpu.SemaphoreType.DMA((12 * count,)),
        ],
        2 * tokens * width * (inner + 2 * GROUP),
        deps=deps,
    )


def add_kernel(left, right, deps):
    def body(left, right, made):
        made[...] = add_low(left[...], right[...])

    return run_kernel(
        body,
        "add_kernel",
        [(left, "v"), (right, "v")],
        [(left.shape, BF16, "v")],
        [],
        left.size,
        deps=deps,
    )[0]


def input_backward(hidden, own, other, residual_grad, vectors, deps):
    tokens, width = hidden.shape

    def body(hidden, own, other, residual_grad, vectors, input_grad, low_grad, sums):
        sums[...] = jnp.zeros_like(sums)

        @pl.loop(0, tokens // ROWS)
        def _(i):
            part = pl.ds(pl.multiple_of(i * ROWS, ROWS), ROWS)
            grad = own[part, :] + other[part, :].astype(F32)
            back, unit = norm_back(hidden[part, :].astype(F32), vectors[0:1, :], grad)
            sums[0:1, :] += column_sum(grad * unit)
            sums[1:2, :] += column_sum(grad)
            back = residual_grad[part, :] + back
            input_grad[part, :] = back
            low_grad[part, :] = back.astype(BF16)

    return run_kernel(
        body,
        "input_backward",
        [(hidden, "v"), (own, "v"), (other, "v"), (residual_grad, "v"), (vectors, "v")],
        [((tokens, width), F32, "v"), ((tokens, width), BF16, "v"), ((8, width), F32, "v")],
        [],
        20 * tokens * width,
        deps=deps,
    )


def swap(value, axis, bit):
    count = lax.axis_size(axis)
    return lax.ppermute(value, axis, [(i, i ^ bit) for i in range(count)])


def add_low(left, right):
    return (left.astype(F32) + right.astype(F32)).astype(BF16)


def gather_blocks(halves, bits):
    places = [1 << i for i in range(len(bits))]
    held, stages = {}, ([], [], [])
    for h, value in enumerate(halves):
        order = list(zip(bits, places))
        order = order if h == 0 else order[::-1]
        blocks = {0: value}
        for hop, (bit, place) in enumerate(order):
            for k in list(blocks):
                blocks[k ^ place] = swap(blocks[k], "fsdp", bit)
                stages[0 if hop == 0 else 1 if k == 0 else 2].append(blocks[k ^ place])
        for k in blocks:
            held[k, h] = blocks[k]
    return [held[k, h] for k in range(1 << len(bits)) for h in range(2)], stages


def scatter_blocks(groups, bits, deps=()):
    results, stages, groups = [], [[] for _ in bits], list(groups)
    for h in range(2):
        held = [groups.pop(0) for _ in range(len(bits) + 1)]
        for hop, bit in enumerate(bits if h == 0 else bits[::-1]):
            far = swap(held.pop(0), "fsdp", bit)
            stages[hop].append(far)
            at = 0
            for i, value in enumerate(held):
                if deps and hop < len(deps) and i == len(held) - 1:
                    held[i] = add_kernel(value, far[at : at + value.shape[0]], deps[hop])
                else:
                    held[i] = add_low(value, far[at : at + value.shape[0]])
                at += value.shape[0]
        results.append(held[0])
    return results, stages


def sum_line(shares, parts=1):
    even = lax.axis_index("seq") % 2 == 0
    low, high = shares
    near = swap(pick(even, high, low), "seq", 1)
    value = add_low(pick(even, low, high), near)
    size = value.shape[0] // parts
    cut = [value[i * size : (i + 1) * size] for i in range(parts)]
    across = [swap(v, "seq", 2) for v in cut]
    value = jnp.concatenate([add_low(v, far) for v, far in zip(cut, across)], axis=0)
    back = swap(value, "seq", 1)
    return [pick(even, value, back), pick(even, back, value)], (near, across, back)


def pick(flag, first, second):
    return jnp.where(flag, first, second)


def side_pick(core, low, high):
    return jnp.where(core == 0, low, high), jnp.where(core == 0, high, low)


def pack_mix(params, mix, out, vectors, scal):
    rows, count = params
    width = out.shape[1]
    lanes = width // (2 * count)
    half = rows // 2
    extra = vectors.shape[0]

    def body(scal, mix, out, vectors, *made):
        core = scal[3]
        for h in range(2):
            kept, sent = made[h], made[2 + h]
            for t in range(3):
                sides = []
                for s in range(2):
                    blocks = range(h * count // 2, (h + 1) * count // 2)
                    at = [t * width + (2 * b + s) * lanes for b in blocks]
                    sides.append(jnp.concatenate([mix[:, i : i + lanes] for i in at], axis=1))
                part = slice(t * rows, (t + 1) * rows)
                kept[part, :], sent[part, :] = side_pick(core, *sides)
            for j in range(2):
                columns = slice((2 * h + j) * GROUP, (2 * h + j + 1) * GROUP)
                part = slice(3 * rows + j * half, 3 * rows + (j + 1) * half)
                kept[part, :], sent[part, :] = side_pick(
                    core, out[:half, columns], out[half:, columns]
                )
            for target in (kept, sent):
                target[4 * rows :, :] = vectors[...]

    return run_kernel(
        body,
        "pack_mix",
        [(scal, "s"), (mix, "v"), (out, "v"), (vectors, "v")],
        [((4 * rows + extra, GROUP), BF16, "v")] * 4,
        [],
        8 * rows * width,
    )


def pack_feed(params, up, down, scal, deps):
    rows, count = params
    inner, width = up.shape[1], down.shape[1]
    lanes = inner // (2 * count)
    wide, narrow = inner // 8, width // 2

    def body(scal, up, down, *made):
        core = scal[3]
        for h in range(2):
            kept, sent = made[h], made[2 + h]
            for j in range(2):
                sides = []
                for s in range(2):
                    first = (2 * h + j) * wide // lanes
                    at = [(2 * (first + q) + s) * lanes for q in range(wide // lanes)]
                    sides.append(jnp.concatenate([up[:, i : i + lanes] for i in at], axis=1))
                part = slice(j * rows, (j + 1) * rows)
                kept[part, :], sent[part, :] = side_pick(core, *sides)
            columns = slice(h * narrow, (h + 1) * narrow)
            part = slice(2 * rows, 4 * rows)
            kept[part, :], sent[part, :] = side_pick(
                core, down[: 2 * rows, columns], down[2 * rows :, columns]
            )

    return run_kernel(
        body,
        "pack_feed",
        [(scal, "s"), (up, "v"), (down, "v")],
        [((4 * rows, wide), BF16, "v")] * 4,
        [],
        8 * rows * inner,
        deps=deps,
    )


def sort_layers(keep, far, scal, deps):
    def body(scal, keep0, keep1, far0, far1, *made):
        for h, (mine, other) in enumerate(((keep0, far0), (keep1, far1))):
            made[h][...], made[2 + h][...] = side_pick(scal[3], mine[...], other[...])

    made = run_kernel(
        body,
        "sort_layers",
        [(scal, "s")] + [(v, "v") for v in keep + far],
        [(v.shape, BF16, "v") for v in keep + far],
        [],
        4 * keep[0].size,
        deps=deps,
    )
    return [made[:2], made[2:]]


def take_vectors(params, pieces, scal):
    rows, count = params
    width = rows * count
    first = 4 * rows
    extra = pieces[0].shape[0] - first

    def body(scal, *rest):
        pieces, (made, up_bias, mix_bias, held, sems) = rest[:count], rest[count:]
        pairs = [
            (pieces[k].at[first : first + extra, 0:rows], held.at[:, block_rows(scal, k, rows)])
            for k in range(count)
        ]
        wait_all(start_all(pairs, sems))
        made[...] = held[...].astype(F32)
        low = scal[3] == 0
        half = rows // 2
        for b in range(count):
            at = b * rows
            for j in range(2):
                columns = slice((2 * b + j) * rows, (2 * b + j + 1) * rows)
                up_bias[:, columns] = jnp.where(
                    low, made[10 + j : 11 + j, at : at + rows], made[12 + j : 13 + j, at : at + rows]
                )
        for index, t in ((2, 0), (3, 2)):
            row = made[index : index + 1, :]
            parts = [
                jnp.where(
                    low,
                    row[:, b * rows : b * rows + half],
                    row[:, b * rows + half : (b + 1) * rows],
                )
                for b in range(count)
            ]
            joint = jnp.concatenate(parts, axis=1)
            for h in range(2):
                at = (3 * h + t) * GROUP
                mix_bias[:, at : at + GROUP] = joint[:, h * GROUP : (h + 1) * GROUP]
        for h in range(2):
            at = (3 * h + 1) * GROUP
            mix_bias[:, at : at + GROUP] = jnp.zeros((1, GROUP), F32)

    return run_kernel(
        body,
        "take_vectors",
        [(scal, "s")] + [(pieces[2 * k], "a") for k in range(count)],
        [((extra, width), F32, "v"), ((1, 2 * width), F32, "v"), ((1, 6 * GROUP), F32, "v")],
        [pltpu.VMEM((extra, width), BF16), pltpu.SemaphoreType.DMA((count,))],
        width,
    )


def unpack_mix(params, own, far, scal, dtype):
    rows, count = params
    width = rows * count
    lanes = width // (2 * count)
    half = rows // 2
    extra = own[0].shape[0] - 4 * rows

    def body(scal, own0, own1, far0, far1, mix, out, vectors):
        for h, (mine, other) in enumerate(((own0, far0), (own1, far1))):
            for t in range(3):
                part = slice(t * rows, (t + 1) * rows)
                for s, value in enumerate(side_pick(scal[3], mine[part, :], other[part, :])):
                    value = value.astype(dtype)
                    for q in range(count // 2):
                        at = t * width + (2 * (h * count // 2 + q) + s) * lanes
                        mix[:, at : at + lanes] = value[:, q * lanes : (q + 1) * lanes]
            for j in range(2):
                part = slice(3 * rows + j * half, 3 * rows + (j + 1) * half)
                columns = slice((2 * h + j) * GROUP, (2 * h + j + 1) * GROUP)
                for s, value in enumerate(side_pick(scal[3], mine[part, :], other[part, :])):
                    out[s * half : (s + 1) * half, columns] = value.astype(dtype)
        sides = side_pick(scal[3], own0[4 * rows :, :], far0[4 * rows :, :])
        for s, value in enumerate(sides):
            vectors[s * extra : (s + 1) * extra, :] = value.astype(F32)

    return run_kernel(
        body,
        "unpack_mix",
        [(scal, "s")] + [(v, "v") for v in own + far],
        [
            ((rows, 3 * width), dtype, "v"),
            ((rows, width), dtype, "v"),
            ((2 * extra, GROUP), F32, "v"),
        ],
        [],
        8 * rows * width,
    )


def unpack_feed(params, own, far, scal, dtype):
    rows, count = params
    width = rows * count
    wide = own[0].shape[1]
    inner = 8 * wide
    lanes = inner // (2 * count)

    def body(scal, own0, own1, far0, far1, up, down):
        for h, (mine, other) in enumerate(((own0, far0), (own1, far1))):
            for j in range(2):
                part = slice(j * rows, (j + 1) * rows)
                for s, value in enumerate(side_pick(scal[3], mine[part, :], other[part, :])):
                    value = value.astype(dtype)
                    for q in range(wide // lanes):
                        at = (2 * ((2 * h + j) * wide // lanes + q) + s) * lanes
                        up[:, at : at + lanes] = value[:, q * lanes : (q + 1) * lanes]
            part = slice(2 * rows, 4 * rows)
            for s, value in enumerate(side_pick(scal[3], mine[part, :], other[part, :])):
                at = s * 2 * rows
                down[at : at + 2 * rows, h * wide : (h + 1) * wide] = value.astype(dtype)

    return run_kernel(
        body,
        "unpack_feed",
        [(scal, "s")] + [(v, "v") for v in own + far],
        [((rows, inner), dtype, "v"), ((4 * rows, width), dtype, "v")],
        [],
        8 * rows * inner,
    )


def body(activations, cotangent, lengths, *weights):
    mixgain, mixshift, mixweight, mixbias, outweight, outbias, mixscale = weights[:7]
    feedgain, feedshift, upweight, upbias, downweight, downbias, feedscale = weights[7:]
    core, line, spot = (lax.axis_index(a) for a in ("section", "seq", "fsdp"))
    first = core == 0
    parity, micro = line % 2, line // 2
    shards = lax.axis_size("fsdp")
    width = activations.shape[-1]
    inner = upbias.shape[1] * shards
    base_rows = width // shards

    joined, rows = 0, base_rows
    while rows // 2 < HEAD_DIM:
        joined, rows = joined + 1, rows * 2
    count = shards >> joined
    bits = [1 << (joined + i) for i in range(count.bit_length() - 1)]
    params = (rows, count)
    block = spot >> joined

    def join(value, axis=0):
        for i in range(joined):
            far = swap(value, "fsdp", 1 << i)
            upper = ((spot >> i) & 1) == 1
            value = jnp.concatenate([pick(upper, far, value), pick(upper, value, far)], axis=axis)
        return value

    def unjoin(value):
        for i in reversed(range(joined)):
            half = value.shape[0] // 2
            upper = ((spot >> i) & 1) == 1
            low, high = value[:half], value[half:]
            value = add_low(pick(upper, high, low), swap(pick(upper, low, high), "fsdp", 1 << i))
        return value.astype(F32)[None]

    low_micro = micro == 0
    length = pick(low_micro, lengths[0, 0], lengths[1, 0])
    scal = jnp.stack([block, parity, length, core]).astype(jnp.int32)

    def spread(packs, deps):
        far = [swap(v, "section", 1) for v in packs[2:]]
        return sort_layers(list(packs[:2]), far, scal, deps)

    tokens = activations.shape[2]

    def to_pair(value):
        keep = pick(low_micro, value[0, 0], value[1, 0])
        far = swap(pick(low_micro, value[1, 0], value[0, 0]), "seq", 2)
        made = jnp.concatenate([pick(low_micro, keep, far), pick(low_micro, far, keep)], axis=0)
        return made, far

    hidden, arrived = to_pair(activations)
    incoming, _ = to_pair(cotangent)

    vectors = jnp.stack(
        [mixgain[0], mixshift[0], mixbias[0, 0], mixbias[0, 1], outbias[0], mixscale[0]]
        + [feedgain[0], feedshift[0], downbias[0], feedscale[0]]
    )
    vectors = jnp.concatenate(
        [join(vectors, 1), join(upbias[0]).reshape(4, rows), jnp.zeros((2, rows), BF16)], axis=0
    )
    if rows < GROUP:
        vectors = jnp.concatenate([vectors, jnp.zeros((16, GROUP - rows), BF16)], axis=1)
    packs = pack_mix(params, join(mixweight[0]), join(outweight[0]), vectors, scal)
    mix_parts = [gather_blocks(halves, bits) for halves in spread(packs, [])]
    mix_pieces, mix_stages = zip(*mix_parts)
    packs = pack_feed(params, join(upweight[0]), join(downweight[0]), scal, [])
    ready = sum(mix_stages[0], []) + [arrived]
    feed_parts = [gather_blocks(halves, bits) for halves in spread(packs, ready)]
    feed_pieces, feed_stages = zip(*feed_parts)

    def send_rows(value):
        return pick(low_micro, value[tokens:], value[:tokens]).astype(BF16)

    def send_layer(sent, layer):
        count = lax.axis_size("seq")
        moves = [(layer * count + i, layer * count + (i ^ 2)) for i in range(count)]
        return lax.ppermute(sent, ("section", "seq"), moves)

    def from_pair(value, far):
        far = far.astype(value.dtype)
        keep = pick(low_micro, value[:tokens], value[tokens:])
        return jnp.stack([pick(low_micro, keep, far), pick(low_micro, far, keep)])[None, :, None]

    result_far = []
    kept, results = [], []
    for layer in range(2):
        pieces, feeds = mix_pieces[layer], feed_pieces[layer]
        vectors, up_bias, mix_bias = take_vectors(params, pieces, scal)
        normed, keep, send = mix_forward(
            params, hidden, vectors, mix_bias, scal, pieces, result_far
        )
        other = swap(send, "seq", 1)
        out_keep, out_send, peaks = attend_forward(
            keep, other, scal,
            feed_stages[layer][0] + feed_stages[layer][1],
        )
        out_other = swap(out_send, "seq", 1)
        mixed, own, send = out_forward(
            params, out_keep, out_other, scal, pieces, width,
            feed_stages[layer][2] + ([incoming] if layer == 0 else []),
        )
        far = swap(send, "section", 1)
        branch, residual, normed_two, active, slope, own, send = feed_forward(
            params, hidden, own, far, vectors, up_bias, scal, feeds,
            [],
        )
        far = swap(send, "section", 1)
        kept.append(
            (hidden, normed, keep, other, peaks, mixed, branch, residual, normed_two, active)
            + (slope, own, far, vectors)
        )
        hidden = layer_result(
            residual, own, far, vectors,
            sum(mix_stages[1], []) if layer == 0 else [],
        )
        results.append(hidden)
        if layer == 0:
            result_far = [send_layer(send_rows(hidden), 0)]

    result_far.append(send_layer(send_rows(results[1]), 1))
    section_output = from_pair(pick(first, *results), pick(first, *result_far))
    gradients, mix_shares, feed_shares = [None] * 2, [None] * 2, [None] * 2
    in_sums, waits = [], {"out": [result_far[1]]}
    for layer in (1, 0):
        pieces, feeds = mix_pieces[layer], feed_pieces[layer]
        hidden, normed, keep, other, peaks, mixed, branch, residual, normed_two, active = kept[
            layer
        ][:10]
        slope, branch_own, branch_far, vectors = kept[layer][10:]
        lower, up_grad, up_sum, own, send = feed_backward(
            params, incoming, vectors, slope, scal, feeds, waits.get("lower", [])
        )
        far = swap(send, "section", 1)
        feed_grads = feed_weights(
            params, active, lower, normed_two, up_grad, scal, waits.get("feed", [branch_far]) + [far],
        )
        feed_share, feed_hops = scatter_blocks(feed_grads, bits)
        feed_shares[layer], feed_moved = sum_line(feed_share)
        feed_sum = feed_sums(incoming, branch_own, branch_far, vectors, lower)
        residual_grad, branch_grad, grad_keep, grad_send, out_sum = out_backward(
            params, incoming, residual, own, far, branch, vectors, scal, pieces,
            [feed_grads[0]] + waits.get("out", []),
        )
        grad_other = swap(grad_send, "seq", 1)
        triple_keep, triple_send = attend_backward(
            keep, other, grad_keep, grad_other, peaks, scal, waits.get("attend", [])
        )
        triple_other = swap(triple_send, "seq", 1)
        triple, own, send = mix_backward(
            params, triple_keep, triple_other, scal, pieces, width,
            waits.get("mix", []) + feed_hops[0],
        )
        far = swap(send, "section", 1)
        input_grad, incoming, in_sum = input_backward(
            hidden, own, far, residual_grad, vectors, waits.get("input", [])
        )
        gradients[layer] = input_grad
        in_sums.append(in_sum)
        after = []
        if layer == 0:
            gradient_far.append(send_layer(send_rows(input_grad), 0))
            after = [[feed_moved[0]], feed_moved[1]]
        if layer == 1:
            gradient_far = [send_layer(send_rows(input_grad), 1)]
        grads = mix_weights(
            params, normed, triple, mixed, branch_grad,
            (in_sums if layer == 0 else []) + [out_sum, feed_sum, up_sum], scal,
            waits.get("weights", []) + (feed_hops[1] if layer == 0 else []),
        )
        mix_share, mix_hops = scatter_blocks(grads, bits, after)
        mix_shares[layer], mix_moved = sum_line(mix_share)
        waits = {
            "feed": gradient_far + feed_hops[-1] + sum(mix_hops, []) + [feed_moved[0]],
            "out": [mix_moved[0]],
            "mix": feed_moved[1],
            "weights": [feed_moved[2]] + mix_moved[1],
        }

    first_rows = mix_shares[0][0][4 * rows :]

    def collect(unpack, shares):
        own = [pick(first, low, high) for low, high in zip(*shares)]
        far = [swap(pick(first, high, low), "section", 1) for low, high in zip(*shares)]
        return unpack(params, own, far, scal, BF16 if joined else F32)

    up_weight, down_weight = (unjoin(v) for v in collect(unpack_feed, feed_shares))
    *made, sums = collect(unpack_mix, mix_shares)
    mix_total, out_total = (unjoin(v) for v in made)

    extra = sums.shape[0] // 2
    sums = sums[:, :rows].reshape(2, extra, rows)
    place = spot & ((1 << joined) - 1)

    def own_part(value):
        size = value.shape[-1] >> joined
        return lax.dynamic_slice_in_dim(value, place * size, size, axis=value.ndim - 1)

    own_sums = pick(first, sums[0], sums[1])
    later = first_rows[11:13, :rows].astype(F32)
    whole = jnp.concatenate([pick(first, own_sums[:2], later), own_sums[2:8]], axis=0)
    whole = own_part(whole)[:, None]
    up_total = own_part(sums[:, 8:10].reshape(1, 4 * rows))
    bias_total = sums[:, 10].reshape(2, 2, rows // 2).transpose(1, 0, 2).reshape(2, rows)
    bias_total = own_part(bias_total)[None]

    return (
        section_output,
        from_pair(pick(first, *gradients), pick(first, *gradient_far[::-1])),
        whole[0],
        whole[1],
        mix_total,
        bias_total,
        out_total,
        whole[5],
        whole[4],
        whole[2],
        whole[3],
        up_weight,
        up_total,
        down_weight,
        whole[7],
        whole[6],
    )


def solution(mesh):
    rowed, flat = P("section", "fsdp", None), P("section", "fsdp")
    image = P(None, "fsdp", "seq", None)
    bias = P("section", None, "fsdp")
    kept = P("section", None, "fsdp", "seq", None)
    params = (flat, flat, rowed, bias, rowed, flat, flat, flat, flat, rowed, flat, rowed, flat, flat)
    return jax.shard_map(
        body,
        mesh=mesh,
        in_specs=(image, image, P(None, "fsdp")) + params,
        out_specs=(kept, kept) + params,
        check_vma=False,
    )
```
